32 devices in a mesh: row: 4 (over x, core), col: 8 (over z, y).
Axes of the slice: x: 2, y: 2, z: 4, core: 2. Of those that a mesh axis runs over, the one named last changes fastest.
Arguments:
- tile_data: bfloat16 [1024, 256, 256], P(('row', 'col')), may hold values from 0 to 256
- owner_ids: int32 [1024, 1], P(('row', 'col')), may hold values from 0 to 31, as said below
- tile_spot: int32 [1024], P(('row', 'col')), may hold values from 0 to 255, as said below
- w_init: float32 [16384, 128], P('row'), may hold values from 0 to 3
- h_init: float32 [32768, 128], P('col'), may hold values from 0 to 3
Outputs:
- w_new: float32 [16384, 128], P('row')
- h_new: float32 [32768, 128], P('col')
The draws below stay inside these ranges and needn't reach their ends.
Inputs may be any that keep to these rules, and one draw needn't show every extreme that they name: `owner_ids`: owner index o names block row o // 8 and block column o % 8; among the 32 tiles of one ingest device no owner is named more than 2 times, and in every draw one owner is named exactly 2 times by every ingest device. `tile_spot`: positions may repeat within an owner's block.
All inputs are finite; a program needn't handle non-finite values.
Results may differ from the reference program's by a relative error of at most 0.0046.
Values may be sent and summed in bfloat16 or wider, within the bound.
No kernel may reach another device: no remote copies, remote signals or barrier semaphores. Data moves between devices by JAX's collectives and lax.ppermute only.
A program may use at most 192 MiB of HBM per device.

```python
import math
import jax
import jax.numpy as jnp
from jax import lax

K = 128
TILE = 256
RT = 16
CT = 16
SLOTS = 32
ITERS = 1
CAP = 2
M = 16384
N = 32768
NT = 1024
N_COL = 8
DEVICES = 32


def tile_layout(key):
    popular = jax.random.permutation(jax.random.fold_in(key, 101), DEVICES).astype(jnp.int32)
    jitter = jax.random.randint(jax.random.fold_in(key, 102), (DEVICES, DEVICES), 0, DEVICES, dtype=jnp.int32)
    leader = (popular == DEVICES - 1).astype(jnp.int32) * (4 * DEVICES)
    scores = (popular * 2 + leader)[None, :] + jitter
    labels = jnp.arange(DEVICES, dtype=jnp.int32)
    distinct = scores * DEVICES + labels[None, :]
    ranked = jnp.argsort(-distinct, axis=1, stable=True).astype(jnp.int32)
    counts = jax.random.randint(jax.random.fold_in(key, 103), (DEVICES, DEVICES), (CAP + 1) // 2, CAP + 1, dtype=jnp.int32)
    counts = jnp.where(labels[None, :] == 0, CAP, counts).astype(jnp.int32)
    bounds = jnp.cumsum(counts, axis=1).astype(jnp.int32)
    slot_ids = jnp.arange(SLOTS, dtype=jnp.int32)
    rank_of = jnp.sum((bounds[:, None, :] <= slot_ids[None, :, None]).astype(jnp.int32), axis=2).astype(jnp.int32)
    owners = jnp.take_along_axis(ranked, rank_of, axis=1).astype(jnp.int32)
    places = jax.random.randint(jax.random.fold_in(key, 104), (DEVICES, SLOTS), 0, RT * CT, dtype=jnp.int32)
    return (owners.reshape(NT), places.reshape(NT))


def drawn_factors(key, cutoff, power):
    first_draw = jax.random.uniform(jax.random.fold_in(key, 201), (M, K), jnp.float32)
    second_draw = jax.random.uniform(jax.random.fold_in(key, 202), (N, K), jnp.float32)
    w_base = (jnp.maximum(first_draw - cutoff, 0.0) / (1.0 - cutoff)) ** power
    h_base = (jnp.maximum(second_draw - cutoff, 0.0) / (1.0 - cutoff)) ** power
    return (w_base, h_base)


def draw_tile_data(key, part):
    owners, places = tile_layout(key)
    w_base, h_base = drawn_factors(key, 0.75, 1.0)
    tile_row = owners // N_COL * RT + places // CT
    tile_col = owners % N_COL * CT + places % CT
    row_panels = w_base.reshape(M // TILE, TILE, K)
    col_panels = h_base.reshape(N // TILE, TILE, K)
    noise_key = jax.random.fold_in(key, 301)

    def one_block(block_id):
        offset = block_id * SLOTS
        rows_here = lax.dynamic_slice_in_dim(tile_row, offset, SLOTS, 0)
        cols_here = lax.dynamic_slice_in_dim(tile_col, offset, SLOTS, 0)
        row_part = row_panels[rows_here]
        col_part = col_panels[cols_here]
        planted = jnp.einsum('sik,sjk->sij', row_part, col_part, precision=lax.Precision.HIGHEST)
        block_key = jax.random.fold_in(noise_key, block_id)
        scale_draw = jax.random.uniform(jax.random.fold_in(block_key, 1), planted.shape, jnp.float32)
        extra_draw = jax.random.uniform(jax.random.fold_in(block_key, 2), planted.shape, jnp.float32)
        values = planted * (0.6 + 0.8 * scale_draw) + 0.4 * extra_draw
        return values.astype(jnp.bfloat16)
    blocks = lax.map(one_block, jnp.arange(DEVICES, dtype=jnp.int32))
    return blocks.reshape(NT, TILE, TILE)


def draw_owner_ids(key, part):
    owners, places = tile_layout(key)
    return owners[:, None]


def draw_tile_spot(key, part):
    owners, places = tile_layout(key)
    return places


def draw_w_init(key, part):
    level = math.sqrt(SLOTS / (RT * CT))
    w_base, h_base = drawn_factors(key, 0.75, 1.0)
    spread = 0.5 + jax.random.uniform(jax.random.fold_in(key, 401), (M, K), jnp.float32)
    return (w_base * spread * level).astype(jnp.float32)


def draw_h_init(key, part):
    level = math.sqrt(SLOTS / (RT * CT))
    w_base, h_base = drawn_factors(key, 0.75, 1.0)
    spread = 0.5 + jax.random.uniform(jax.random.fold_in(key, 402), (N, K), jnp.float32)
    return (h_base * spread * level).astype(jnp.float32)


def setup_inputs(seed: int = 0) -> dict:
    seeds = jax.random.split(jax.random.key(seed), 6)
    tile_data = draw_tile_data(jax.random.fold_in(seeds[5], 71), 0)
    owner_ids = draw_owner_ids(jax.random.fold_in(seeds[5], 71), 0)
    tile_spot = draw_tile_spot(jax.random.fold_in(seeds[5], 71), 0)
    w_init = draw_w_init(jax.random.fold_in(seeds[5], 71), 0)
    h_init = draw_h_init(jax.random.fold_in(seeds[5], 71), 0)
    return dict(tile_data=tile_data, owner_ids=owner_ids, tile_spot=tile_spot, w_init=w_init, h_init=h_init)


EPS = 1e-6
RIDGE = 1.0
HIGH = lax.Precision.HIGHEST


def sweep_columns(factor, product, gram_mat):
    def update(column, current):
        gram_col = lax.dynamic_index_in_dim(gram_mat, column, 1, keepdims=False)
        diag_val = lax.dynamic_index_in_dim(gram_col, column, 0, keepdims=False)
        before_col = lax.dynamic_index_in_dim(current, column, 1, keepdims=False)
        prod_col = lax.dynamic_index_in_dim(product, column, 1, keepdims=False)
        numer = prod_col - jnp.dot(current, gram_col, precision=HIGH) + before_col * diag_val
        updated = jnp.maximum(numer / (diag_val + RIDGE), EPS)
        return lax.dynamic_update_index_in_dim(current, updated, column, 1)
    return lax.fori_loop(0, factor.shape[1], update, factor)


def accumulate(tile_data, target, source, factor, blocks, flipped):
    count = tile_data.shape[0]
    tile_size = tile_data.shape[1]
    rank_size = factor.shape[1]
    panels = factor.reshape(-1, tile_size, rank_size)
    stride = math.gcd(count, 256)
    pattern = "bji,bjk->bik" if flipped else "bij,bjk->bik"

    def advance(running, block_id):
        start = block_id * stride
        pieces = lax.dynamic_slice_in_dim(tile_data, start, stride, 0).astype(jnp.float32)
        picked = panels[lax.dynamic_slice_in_dim(source, start, stride, 0)].astype(jnp.float32)
        placed = lax.dynamic_slice_in_dim(target, start, stride, 0)
        terms = jnp.einsum(pattern, pieces, picked, precision=HIGH)
        return running.at[placed].add(terms), None

    running = jnp.zeros((blocks, tile_size, rank_size), jnp.float32)
    running, _ = lax.scan(advance, running, jnp.arange(count // stride, dtype=jnp.int32))
    return running.reshape(blocks * tile_size, rank_size)


def reference(tile_data, owner_ids, tile_spot, w_init, h_init):
    target = owner_ids[:, 0]
    tile_row = (target // N_COL) * RT + tile_spot // CT
    tile_col = (target % N_COL) * CT + tile_spot % CT
    w_factor = w_init
    h_factor = h_init
    for sweep_id in range(ITERS):
        h_low = h_factor.astype(jnp.bfloat16)
        prod_w = accumulate(tile_data, tile_row, tile_col, h_low, M // TILE, False)
        gram_h = jnp.dot(h_factor.T, h_factor, preferred_element_type=jnp.float32, precision=HIGH)
        w_factor = sweep_columns(w_factor, prod_w, gram_h)
        w_low = w_factor.astype(jnp.bfloat16)
        prod_h = accumulate(tile_data, tile_col, tile_row, w_low, N // TILE, True)
        gram_w = jnp.dot(w_factor.T, w_factor, preferred_element_type=jnp.float32, precision=HIGH)
        h_factor = sweep_columns(h_factor, prod_h, gram_w)
    return w_factor, h_factor
```

```python
import jax
import jax.numpy as jnp
from jax import lax
from jax.experimental import pallas as pl
from jax.experimental.pallas import tpu as pltpu
from jax.sharding import Mesh
from jax.sharding import PartitionSpec as P

CT = 16
CAP = 2
EPS = 1e-06
RIDGE = 1.0
HIGH = lax.Precision.HIGHEST
F32 = jnp.float32
LINK = jnp.float16
STEP = 16
VMEM_LIMIT = 48 * 2**20


def params():
    return pltpu.CompilerParams(vmem_limit_bytes=VMEM_LIMIT)


def pack(slot, tile_data, slots):
    count, size = tile_data.shape[0], tile_data.shape[1]

    def kernel(slot_ref, tiles_ref, out_ref, sems):
        copies = [
            pltpu.make_async_copy(tiles_ref.at[s], out_ref.at[slot_ref[s]], sems.at[s])
            for s in range(count)
        ]
        for copy in copies:
            copy.start()
        for copy in copies:
            copy.wait()

    return pl.pallas_call(
        kernel,
        out_shape=jax.ShapeDtypeStruct((slots, size, size), tile_data.dtype),
        in_specs=[pl.BlockSpec(memory_space=pltpu.SMEM), pl.BlockSpec(memory_space=pl.ANY)],
        out_specs=pl.BlockSpec(memory_space=pl.ANY),
        scratch_shapes=[pltpu.SemaphoreType.DMA((count,))],
        compiler_params=params(),
    )(slot, tile_data)


def row_products(inbox, meta, first, panels, chunks):
    senders, held, size, _ = inbox.shape
    groups, rank, length = panels.shape
    width = length // chunks
    per_chunk = width // size

    def kernel(meta_ref, first_ref, tile_ref, panel_ref, out_ref):
        sender = pl.program_id(0)

        @pl.when(sender == 0)
        def _():
            out_ref[...] = jnp.zeros_like(out_ref)

        for slot in range(held):
            spot = meta_ref[sender * held + slot] - 1

            @pl.when(spot >= 0)
            def _():
                trow, tcol = spot // CT, spot % CT
                group = lax.rem(first_ref[0] + groups - slot // CAP, groups)
                panel = panel_ref[group, :, pl.ds(pl.multiple_of(tcol * size, size), size)]
                term = lax.dot_general(
                    panel, tile_ref[0, slot], (((1,), (1,)), ((), ())), preferred_element_type=F32
                )
                lanes = pl.ds(pl.multiple_of((trow % per_chunk) * size, size), size)
                out_ref[trow // per_chunk, :, lanes] += term

    return pl.pallas_call(
        kernel,
        out_shape=jax.ShapeDtypeStruct((chunks, rank, width), F32),
        grid_spec=pltpu.PrefetchScalarGridSpec(
            num_scalar_prefetch=2,
            grid=(senders,),
            in_specs=[
                pl.BlockSpec((1, held, size, size), lambda i, *_: (i, 0, 0, 0)),
                pl.BlockSpec((groups, rank, length), lambda i, *_: (0, 0, 0)),
            ],
            out_specs=pl.BlockSpec((chunks, rank, width), lambda i, *_: (0, 0, 0)),
        ),
        compiler_params=params(),
    )(meta, first, inbox, panels)


def column_products(inbox, meta, me, panels, owners):
    senders, held, size, _ = inbox.shape
    chunks, rank, width = panels.shape
    per_chunk = width // size
    length = chunks * width
    groups = held // CAP
    out_width = length // owners
    per_out = out_width // size
    half = owners // 2

    def kernel(meta_ref, me_ref, tile_ref, panel_ref, keep_ref, send_ref):
        sender = pl.program_id(0)

        @pl.when(sender == 0)
        def _():
            keep_ref[...] = jnp.zeros_like(keep_ref)
            send_ref[...] = jnp.zeros_like(send_ref)

        for slot in range(held):
            spot = meta_ref[sender * held + slot] - 1

            @pl.when(spot >= 0)
            def _():
                trow, tcol = spot // CT, spot % CT
                lanes = pl.ds(pl.multiple_of((trow % per_chunk) * size, size), size)
                panel = panel_ref[trow // per_chunk, :, lanes]
                term = lax.dot_general(
                    panel, tile_ref[0, slot], (((1,), (0,)), ((), ())), preferred_element_type=F32
                )
                owner = tcol // per_out
                far = owner // 2 ^ me_ref[0] // 2
                other = (owner ^ me_ref[0]) % 2
                place = pl.ds(pl.multiple_of((tcol % per_out) * size, size), size)

                @pl.when(other == 0)
                def _():
                    keep_ref[far, slot // CAP, :, place] += term

                @pl.when(other == 1)
                def _():
                    send_ref[far, slot // CAP, :, place] += term

    shape = (half, groups, rank, out_width)
    out_spec = pl.BlockSpec(shape, lambda i, *_: (0, 0, 0, 0))
    return pl.pallas_call(
        kernel,
        out_shape=[jax.ShapeDtypeStruct(shape, F32)] * 2,
        grid_spec=pltpu.PrefetchScalarGridSpec(
            num_scalar_prefetch=2,
            grid=(senders,),
            in_specs=[
                pl.BlockSpec((1, held, size, size), lambda i, *_: (i, 0, 0, 0)),
                pl.BlockSpec((chunks, rank, width), lambda i, *_: (0, 0, 0)),
            ],
            out_specs=[out_spec, out_spec],
        ),
        compiler_params=params(),
    )(meta, me, inbox, panels)


def sweep_block(factor, product, gram, left_ref):
    rank = factor.shape[0]
    left_ref[...] = product - lax.dot_general(
        gram, factor, (((0,), (0,)), ((), ())), precision=HIGH, preferred_element_type=F32
    )
    outs = []
    for lead in range(0, rank, STEP):
        before = factor[lead : lead + STEP]
        block = gram[lead : lead + STEP, lead : lead + STEP]
        left = left_ref[lead : lead + STEP]
        news, moves = [], []
        for k in range(STEP):
            diag = block[k : k + 1, k : k + 1]
            old = before[k : k + 1]
            new = jnp.maximum((left[k : k + 1] + old * diag) / (diag + RIDGE), EPS)
            move = new - old
            news.append(new)
            moves.append(move)
            if k + 1 < STEP:
                left = left - jnp.transpose(block[k : k + 1, :]) * move
        outs.append(jnp.concatenate(news, axis=0))
        if lead + STEP < rank:
            moved = jnp.concatenate(moves, axis=0)
            left_ref[lead + STEP :] -= lax.dot_general(
                gram[lead : lead + STEP, lead + STEP :],
                moved,
                (((0,), (0,)), ((), ())),
                precision=HIGH,
                preferred_element_type=F32,
            )
    return jnp.concatenate(outs, axis=0)


def sweep_w(factor, product, gram):
    rank, width = factor.shape

    def kernel(factor_ref, product_ref, gram_ref, low_ref, own_ref, left_ref):
        new = sweep_block(factor_ref[...], product_ref[...], gram_ref[...], left_ref)
        low_ref[...] = new.astype(jnp.bfloat16)
        own_ref[...] = lax.dot_general(
            new, new, (((1,), (1,)), ((), ())), precision=HIGH, preferred_element_type=F32
        )

    return pl.pallas_call(
        kernel,
        out_shape=[
            jax.ShapeDtypeStruct((rank, width), jnp.bfloat16),
            jax.ShapeDtypeStruct((rank, rank), F32),
        ],
        scratch_shapes=[pltpu.VMEM((rank, width), F32)],
        compiler_params=params(),
    )(factor, product, gram)


def sweep_h(factor, product, gram):
    rank, width = factor.shape

    def kernel(factor_ref, product_ref, gram_ref, low_ref, left_ref):
        new = sweep_block(factor_ref[...], product_ref[...], gram_ref[...], left_ref)
        low_ref[...] = jnp.transpose(new).astype(jnp.bfloat16)

    return pl.pallas_call(
        kernel,
        out_shape=jax.ShapeDtypeStruct((width, rank), jnp.bfloat16),
        scratch_shapes=[pltpu.VMEM((rank, width), F32)],
        compiler_params=params(),
    )(factor, product, gram)


def swap(x, axis, bit):
    size = lax.axis_size(axis)
    return lax.ppermute(x, axis, [(i, i ^ bit) for i in range(size)])


def bits(axis):
    bit = 1
    while bit < lax.axis_size(axis):
        yield bit
        bit *= 2


def everywhere(x, axes, combine):
    for axis in axes:
        for bit in bits(axis):
            x = combine(x, swap(x, axis, bit))
    return x


def local(tile_data, owner_ids, tile_spot, w_init, h_init):
    row_axes, col_axes = ("far", "core"), ("hi", "lo")
    fars, cores = lax.axis_size("far"), lax.axis_size("core")
    his, los = lax.axis_size("hi"), lax.axis_size("lo")
    rows, cols = fars * cores, his * los
    slots = rows * cols * CAP
    size, rank = tile_data.shape[1], w_init.shape[1]
    my_row, my_hi = lax.axis_index(row_axes), lax.axis_index("hi")
    my_col, core = lax.axis_index(col_axes), lax.axis_index("core")

    owner = owner_ids[:, 0]
    same = owner[:, None] == owner[None, :]
    count = owner.shape[0]
    earlier = jnp.arange(count)[None, :] < jnp.arange(count)[:, None]
    nth = jnp.sum((same & earlier).astype(jnp.int32), axis=1)
    o_row, o_col = owner // cols, owner % cols
    slot = ((o_row * los + o_col % los) * his + o_col // los) * CAP + nth
    marks = slot[:, None] == jnp.arange(slots, dtype=jnp.int32)[None, :]
    meta = jnp.sum(jnp.where(marks, tile_spot[:, None] + 1, 0), axis=0)

    plane = ("far", "core", "lo")
    peers = rows * los
    outbox = pack(slot, tile_data, slots).reshape(peers, his * CAP, size, size)
    inbox = lax.all_to_all(outbox, plane, split_axis=0, concat_axis=0, tiled=True)
    meta = lax.all_to_all(
        meta.reshape(peers, his * CAP), plane, split_axis=0, concat_axis=0, tiled=True
    ).reshape(-1)

    h_t = h_init.T
    low = h_t.astype(jnp.bfloat16)
    piece = lax.dynamic_slice_in_dim(low, core * (rank // 2), rank // 2, 0)
    pieces = [piece] + [
        lax.ppermute(piece, "hi", [(i, (i + shift) % his) for i in range(his)])
        for shift in range(1, his)
    ]
    mine = jnp.stack(pieces)
    theirs = swap(mine, "core", 1)
    panels = jnp.where(
        core == 0,
        jnp.concatenate([mine, theirs], axis=1),
        jnp.concatenate([theirs, mine], axis=1),
    )

    gram_h = lax.dot_general(h_t, h_t, (((1,), (1,)), ((), ())), precision=HIGH)
    gram_h = everywhere(gram_h, col_axes, jnp.add)
    peak = jnp.max(tile_data.astype(F32))
    peak = everywhere(jnp.full((8, 128), peak), row_axes + col_axes, jnp.maximum)[0, 0]
    peak = jnp.maximum(peak, 1e-20)

    def scale_for(gram, terms):
        norm = jnp.sqrt(jnp.maximum(jnp.max(gram), 1e-30))
        return 32768.0 / (terms * size**0.5 * peak * norm)

    up = scale_for(gram_h, slots)
    part = row_products(inbox, meta, my_hi[None].astype(jnp.int32), panels, cols)
    width = part.shape[2]
    got = lax.all_to_all((part * up).astype(LINK), col_axes, 0, 0, tiled=True)
    product_w = jnp.sum(got.astype(F32), axis=0) / up
    w_t = lax.dynamic_slice_in_dim(w_init, my_col * width, width, 0).T
    w_low, gram_w = sweep_w(w_t, product_w, gram_h)
    w_all = lax.all_to_all(
        jnp.broadcast_to(w_low[None], (cols, rank, width)), col_axes, 0, 0, tiled=True
    )
    gram_w = everywhere(gram_w, row_axes + col_axes, jnp.add)
    w_new = jnp.transpose(w_all, (0, 2, 1)).reshape(cols * width, rank).astype(F32)

    keep, send = column_products(inbox, meta, my_row[None].astype(jnp.int32), w_all, rows)
    keep = keep + swap(send, "core", 1)
    up = scale_for(gram_w, slots * rows * his)
    half = fars // 2
    while half:
        send = (keep[half:] * up).astype(LINK)
        keep = keep[:half] + swap(send, "far", half).astype(F32) / up
        half //= 2
    got = lax.all_to_all((keep[0] * up).astype(LINK), "hi", 0, 0, tiled=True)
    product_h = jnp.sum(got.astype(F32), axis=0) / up
    length = product_h.shape[1]
    own_t = lax.dynamic_slice_in_dim(h_init, my_row * length, length, 0).T
    h_low = sweep_h(own_t, product_h, gram_w)
    h_all = lax.all_to_all(
        jnp.broadcast_to(h_low[None], (rows, length, rank)), row_axes, 0, 0, tiled=True
    )
    return w_new, h_all.reshape(rows * length, rank).astype(F32)


def solution(mesh):
    rows, cols = mesh.shape["row"], mesh.shape["col"]
    his = 4 if cols % 4 == 0 else 1
    shape = (rows // 2, 2, his, cols // his)
    fine = Mesh(mesh.devices.reshape(shape), ("far", "core", "hi", "lo"))
    row, col = ("far", "core"), ("hi", "lo")
    in_specs = (P(row + col, None, None), P(row + col, None), P(row + col), P(row, None), P(col, None))
    out_specs = (P(row, None), P(col, None))
    return jax.shard_map(local, mesh=fine, in_specs=in_specs, out_specs=out_specs, check_vma=False)
```

```python
import jax
import jax.numpy as jnp
from jax import lax
from jax.experimental import pallas as pl
from jax.experimental.pallas import tpu as pltpu
from jax.sharding import Mesh
from jax.sharding import PartitionSpec as P

CT = 16
CAP = 2
EPS = 1e-06
RIDGE = 1.0
HIGH = lax.Precision.HIGHEST
F32 = jnp.float32
LINK = jnp.float16
STEP = 16
VMEM_LIMIT = 48 * 2**20


def params():
    return pltpu.CompilerParams(vmem_limit_bytes=VMEM_LIMIT)


def pack(slot, tile_data, slots):
    count, size = tile_data.shape[0], tile_data.shape[1]

    def kernel(slot_ref, tiles_ref, out_ref, sems):
        copies = [
            pltpu.make_async_copy(tiles_ref.at[s], out_ref.at[slot_ref[s]], sems.at[s])
            for s in range(count)
        ]
        for copy in copies:
            copy.start()
        for copy in copies:
            copy.wait()

    return pl.pallas_call(
        kernel,
        out_shape=jax.ShapeDtypeStruct((slots, size, size), tile_data.dtype),
        in_specs=[pl.BlockSpec(memory_space=pltpu.SMEM), pl.BlockSpec(memory_space=pl.ANY)],
        out_specs=pl.BlockSpec(memory_space=pl.ANY),
        scratch_shapes=[pltpu.SemaphoreType.DMA((count,))],
        compiler_params=params(),
    )(slot, tile_data)


def row_products(inbox, meta, me, pieces, his, los, width):
    senders, held, size, _ = inbox.shape
    part, length = pieces[0].shape
    rank = 2 * part
    per_chunk = width // size

    def kernel(meta_ref, me_ref, tile_ref, *refs):
        piece_refs, (top_ref, bot_ref), (panel_ref, term_ref) = refs[: 2 * his], refs[-4:-2], refs[-2:]
        sender = pl.program_id(0)
        my_core, my_hi, my_lo = me_ref[1], me_ref[2], me_ref[3]

        @pl.when(sender == 0)
        def _():
            top_ref[...] = jnp.zeros_like(top_ref)
            bot_ref[...] = jnp.zeros_like(bot_ref)
            for side in range(2):
                rows = pl.ds(pl.multiple_of((my_core ^ side) * part, part), part)
                for j in range(his):
                    panel_ref[j, rows, :] = piece_refs[side * his + j][...]

        for slot in range(held):
            spot = jnp.maximum(meta_ref[sender, slot] - 1, 0)
            place = pl.ds(pl.multiple_of((spot % CT) * size, size), size)
            term_ref[slot] = lax.dot_general(
                panel_ref[slot // CAP ^ my_hi, :, place],
                tile_ref[0, slot],
                (((1,), (1,)), ((), ())),
                preferred_element_type=F32,
            )

        for slot in range(held):
            spot = meta_ref[sender, slot] - 1

            @pl.when(spot >= 0)
            def _():
                trow = spot // CT
                chunk = trow // per_chunk
                lanes = pl.ds(pl.multiple_of((trow % per_chunk) * size, size), size)
                at = (chunk % los ^ my_lo, chunk // los ^ my_hi)
                top_ref[at[0], at[1], :, lanes] += term_ref[slot, :part]
                bot_ref[at[0], at[1], :, lanes] += term_ref[slot, part:]

    shape = (los, his, part, width)
    piece_spec = pl.BlockSpec((part, length), lambda i, *_: (0, 0))
    out_spec = pl.BlockSpec(shape, lambda i, *_: (0, 0, 0, 0))
    return pl.pallas_call(
        kernel,
        out_shape=[jax.ShapeDtypeStruct(shape, F32)] * 2,
        grid_spec=pltpu.PrefetchScalarGridSpec(
            num_scalar_prefetch=2,
            grid=(senders,),
            in_specs=[pl.BlockSpec((1, held, size, size), lambda i, *_: (i, 0, 0, 0))]
            + [piece_spec] * (2 * his),
            out_specs=[out_spec] * 2,
            scratch_shapes=[
                pltpu.VMEM((his, rank, length), jnp.bfloat16),
                pltpu.VMEM((held, rank, size), F32),
            ],
        ),
        compiler_params=params(),
    )(meta, me, inbox, *pieces)


def column_products(inbox, meta, me, pieces, his, los, fars, out_width):
    senders, held, size, _ = inbox.shape
    rank, width = pieces[0].shape
    part = rank // 2
    per_chunk, per_out = width // size, out_width // size
    chunks = his * los

    def kernel(meta_ref, me_ref, tile_ref, *refs):
        piece_refs, outs, peak_ref = refs[:chunks], refs[chunks : chunks + 4], refs[chunks + 4]
        panel_ref, term_ref = refs[-2:]
        keeps, sends = outs[:2], outs[2:]
        sender = pl.program_id(0)
        my_far, my_core, my_hi, my_lo = (me_ref[i] for i in range(4))

        @pl.when(sender == 0)
        def _():
            for out in outs:
                out[...] = jnp.zeros_like(out)
            top = jnp.zeros((rank, width), jnp.bfloat16)
            for j in range(chunks):
                panel_ref[j] = piece_refs[j][...]
                top = jnp.maximum(top, piece_refs[j][...])
            peak_ref[...] = jnp.full(peak_ref.shape, jnp.max(top.astype(F32)))

        for slot in range(held):
            spot = jnp.maximum(meta_ref[sender, slot] - 1, 0)
            trow = spot // CT
            chunk = trow // per_chunk
            lanes = pl.ds(pl.multiple_of((trow % per_chunk) * size, size), size)
            at = (chunk // los ^ my_hi) * los + (chunk % los ^ my_lo)
            term_ref[slot] = lax.dot_general(
                panel_ref[at, :, lanes],
                tile_ref[0, slot],
                (((1,), (0,)), ((), ())),
                preferred_element_type=F32,
            )

        for slot in range(held):
            spot = meta_ref[sender, slot] - 1
            tcol = spot % CT
            owner = tcol // per_out
            place = pl.ds(pl.multiple_of((tcol % per_out) * size, size), size)
            at = (owner // 2 ^ my_far, slot // CAP ^ my_hi)
            for side, dests in enumerate((keeps, sends)):

                @pl.when((spot >= 0) & ((owner ^ my_core) % 2 == side))
                def _():
                    dests[0][at[0], at[1], :, place] += term_ref[slot, :part]
                    dests[1][at[0], at[1], :, place] += term_ref[slot, part:]

    shape = (fars, his, part, out_width)
    out_spec = pl.BlockSpec(shape, lambda i, *_: (0, 0, 0, 0))
    return pl.pallas_call(
        kernel,
        out_shape=[jax.ShapeDtypeStruct(shape, F32)] * 4 + [jax.ShapeDtypeStruct((8, 128), F32)],
        grid_spec=pltpu.PrefetchScalarGridSpec(
            num_scalar_prefetch=2,
            grid=(senders,),
            in_specs=[pl.BlockSpec((1, held, size, size), lambda i, *_: (i, 0, 0, 0))]
            + [pl.BlockSpec((rank, width), lambda i, *_: (0, 0))] * chunks,
            out_specs=[out_spec] * 4 + [pl.BlockSpec((8, 128), lambda i, *_: (0, 0))],
            scratch_shapes=[
                pltpu.VMEM((chunks, rank, width), jnp.bfloat16),
                pltpu.VMEM((held, rank, size), F32),
            ],
        ),
        compiler_params=params(),
    )(meta, me, inbox, *pieces)


def assemble(pieces, place, turned):
    count = len(pieces)
    rank, width = pieces[0].shape if turned else pieces[0].shape[::-1]

    def kernel(place_ref, *refs):
        for j in range(count):
            piece = refs[j][...].astype(F32)
            refs[count][j ^ place_ref[0]] = jnp.transpose(piece) if turned else piece

    return pl.pallas_call(
        kernel,
        out_shape=jax.ShapeDtypeStruct((count, width, rank), F32),
        in_specs=[pl.BlockSpec(memory_space=pltpu.SMEM)]
        + [pl.BlockSpec(memory_space=pltpu.VMEM)] * count,
        out_specs=pl.BlockSpec(memory_space=pltpu.VMEM),
        compiler_params=params(),
    )(place, *pieces).reshape(count * width, rank)


def sweep_block(factor, product, gram, left_ref):
    rank = factor.shape[0]
    left_ref[...] = product - lax.dot_general(
        gram, factor, (((0,), (0,)), ((), ())), precision=HIGH, preferred_element_type=F32
    )
    outs = []
    for lead in range(0, rank, STEP):
        before = factor[lead : lead + STEP]
        block = gram[lead : lead + STEP, lead : lead + STEP]
        left = left_ref[lead : lead + STEP]
        news, moves = [], []
        for k in range(STEP):
            diag = block[k : k + 1, k : k + 1]
            old = before[k : k + 1]
            new = jnp.maximum((left[k : k + 1] + old * diag) / (diag + RIDGE), EPS)
            move = new - old
            news.append(new)
            moves.append(move)
            if k + 1 < STEP:
                left = left - jnp.transpose(block[k : k + 1, :]) * move
        outs.append(jnp.concatenate(news, axis=0))
        if lead + STEP < rank:
            moved = jnp.concatenate(moves, axis=0)
            left_ref[lead + STEP :] -= lax.dot_general(
                gram[lead : lead + STEP, lead + STEP :],
                moved,
                (((0,), (0,)), ((), ())),
                precision=HIGH,
                preferred_element_type=F32,
            )
    return jnp.concatenate(outs, axis=0)


def sweep_w(factor, top, bottom, gram):
    rank, width = factor.shape

    def kernel(factor_ref, top_ref, bottom_ref, gram_ref, low_ref, own_ref, left_ref):
        product = jnp.concatenate([top_ref[...], bottom_ref[...]], axis=0)
        new = sweep_block(factor_ref[...], product, gram_ref[...], left_ref)
        low_ref[...] = new.astype(jnp.bfloat16)
        own_ref[...] = lax.dot_general(
            new, new, (((1,), (1,)), ((), ())), precision=HIGH, preferred_element_type=F32
        )

    return pl.pallas_call(
        kernel,
        out_shape=[
            jax.ShapeDtypeStruct((rank, width), jnp.bfloat16),
            jax.ShapeDtypeStruct((rank, rank), F32),
        ],
        scratch_shapes=[pltpu.VMEM((rank, width), F32)],
        compiler_params=params(),
    )(factor, top, bottom, gram)


def sweep_h(factor, top, bottom, gram):
    rank, width = factor.shape

    def kernel(factor_ref, top_ref, bottom_ref, gram_ref, low_ref, left_ref):
        product = jnp.concatenate([top_ref[...], bottom_ref[...]], axis=0)
        new = sweep_block(factor_ref[...], product, gram_ref[...], left_ref)
        low_ref[...] = jnp.transpose(new).astype(jnp.bfloat16)

    return pl.pallas_call(
        kernel,
        out_shape=jax.ShapeDtypeStruct((width, rank), jnp.bfloat16),
        scratch_shapes=[pltpu.VMEM((rank, width), F32)],
        compiler_params=params(),
    )(factor, top, bottom, gram)


def swap(x, axis, bit):
    size = lax.axis_size(axis)
    return lax.ppermute(x, axis, [(i, i ^ bit) for i in range(size)])


def bits(axis):
    bit = 1
    while bit < lax.axis_size(axis):
        yield bit
        bit *= 2


def everywhere(x, axes, combine):
    for axis in axes:
        for bit in bits(axis):
            x = combine(x, swap(x, axis, bit))
    return x


def spread(pieces, axis):
    return [
        piece if j == 0 else swap(piece, axis, j)
        for piece in pieces
        for j in range(lax.axis_size(axis))
    ]


def gather(sums, axis, up, down):
    total = sums[0]
    for j in range(1, lax.axis_size(axis)):
        total = total + swap((sums[j] * up).astype(LINK), axis, j).astype(F32) * down
    return total


def local(tile_data, owner_ids, tile_spot, w_init, h_init):
    row_axes, col_axes = ("far", "core"), ("hi", "lo")
    fars, cores = lax.axis_size("far"), lax.axis_size("core")
    his, los = lax.axis_size("hi"), lax.axis_size("lo")
    rows, cols = fars * cores, his * los
    slots = rows * cols * CAP
    size, rank = tile_data.shape[1], w_init.shape[1]
    width, length = w_init.shape[0] // cols, h_init.shape[0] // rows
    my_row, my_col = lax.axis_index(row_axes), lax.axis_index(col_axes)
    core = lax.axis_index("core")
    me = jnp.stack([lax.axis_index(a) for a in row_axes + col_axes]).astype(jnp.int32)

    owner = owner_ids[:, 0]
    count = owner.shape[0]
    same = owner[:, None] == owner[None, :]
    earlier = jnp.arange(count)[None, :] < jnp.arange(count)[:, None]
    nth = jnp.sum((same & earlier).astype(jnp.int32), axis=1)
    o_row, o_col = owner // cols, owner % cols
    slot = ((o_row * los + o_col % los) * his + o_col // los) * CAP + nth

    plane = ("far", "core", "lo")
    peers, held = rows * los, his * CAP
    outbox = pack(slot, tile_data, slots).reshape(peers, held, size, size)
    inbox = lax.all_to_all(outbox, plane, split_axis=0, concat_axis=0, tiled=True)

    h_t = h_init.T
    piece = lax.dynamic_slice_in_dim(h_t, core * (rank // 2), rank // 2, 0).astype(jnp.bfloat16)
    pieces = spread([piece], "hi")
    pieces += [swap(piece, "core", 1) for piece in pieces]

    gram_h = lax.dot_general(h_t, h_t, (((1,), (1,)), ((), ())), precision=HIGH)
    gram_h = everywhere(gram_h, col_axes, jnp.add)
    peak = everywhere(jnp.full((8, 128), jnp.max(tile_data).astype(F32)), ("hi",), jnp.maximum)[0, 0]
    peak = jnp.ceil(jnp.log2(jnp.maximum(peak, 1e-20))).astype(jnp.int32)
    marks = slot[:, None] == jnp.arange(slots, dtype=jnp.int32)[None, :]
    meta = jnp.sum(jnp.where(marks, tile_spot[:, None] + 1, 0), axis=0).reshape(peers, held)
    meta = jnp.concatenate([meta, jnp.broadcast_to(peak, (peers, 1))], axis=1)
    meta = lax.all_to_all(meta, plane, split_axis=0, concat_axis=0, tiled=True)
    peak = jnp.exp2(jnp.max(meta[:, held]).astype(F32))

    norm = jnp.sqrt(jnp.maximum(jnp.max(gram_h), 1e-30))
    down = slots * size**0.5 * los / 32768.0 * peak * norm
    up = 1.0 / down
    parts = row_products(inbox, meta, me, pieces, his, los, width)
    sums = [gather(gather(part, "lo", up, down), "hi", up, down) for part in parts]
    w_t = lax.dynamic_slice_in_dim(w_init, my_col * width, width, 0).T
    w_low, gram_w = sweep_w(w_t, *sums, gram_h)
    pieces = spread(spread([w_low], "hi"), "lo")
    gram_w = everywhere(gram_w, row_axes + col_axes, jnp.add)

    *parts, high = column_products(inbox, meta, me, pieces, his, los, fars, length)
    w_new = assemble(pieces, my_col[None].astype(jnp.int32), True)
    high = jnp.maximum(everywhere(high, row_axes, jnp.maximum)[0, 0], 1e-20)
    down = slots * rows * size / 32768.0 * peak * high
    up = 1.0 / down
    sums = []
    for keep, send in zip(parts[:2], parts[2:]):
        keep = keep + swap(send, "core", 1)
        half = fars // 2
        while half:
            keep = keep[:half] + swap((keep[half:] * up).astype(LINK), "far", half).astype(F32) * down
            half //= 2
        sums.append(gather(keep[0], "hi", up, down))
    own_t = lax.dynamic_slice_in_dim(h_init, my_row * length, length, 0).T
    h_low = sweep_h(own_t, *sums, gram_w)
    h_new = assemble(spread(spread([h_low], "far"), "core"), my_row[None].astype(jnp.int32), False)
    return w_new, h_new


def solution(mesh):
    rows, cols = mesh.shape["row"], mesh.shape["col"]
    his = 4 if cols % 4 == 0 else 1
    shape = (rows // 2, 2, his, cols // his)
    fine = Mesh(mesh.devices.reshape(shape), ("far", "core", "hi", "lo"))
    row, col = ("far", "core"), ("hi", "lo")
    in_specs = (P(row + col, None, None), P(row + col, None), P(row + col), P(row, None), P(col, None))
    out_specs = (P(row, None), P(col, None))
    return jax.shard_map(local, mesh=fine, in_specs=in_specs, out_specs=out_specs, check_vma=False)
```

```python
import jax
import jax.numpy as jnp
from jax import lax
from jax.experimental import pallas as pl
from jax.experimental.pallas import tpu as pltpu
from jax.sharding import Mesh
from jax.sharding import PartitionSpec as P

CT = 16
CAP = 2
EPS = 1e-06
RIDGE = 1.0
HIGH = lax.Precision.HIGHEST
F32 = jnp.float32
LINK = jnp.float16
STEP = 32
BATCH = 2
PEAK = 256.0
VMEM_LIMIT = 48 * 2**20


def params():
    return pltpu.CompilerParams(vmem_limit_bytes=VMEM_LIMIT)


def pack(slot, tile_data, notes, held):
    count, size = tile_data.shape[0], tile_data.shape[1]
    peers, extra = notes.shape[0], notes.shape[1]

    def kernel(slot_ref, tiles_ref, notes_ref, out_ref, sems):
        copies = []
        for s in range(count):
            rows = pl.ds(pl.multiple_of((slot_ref[s] % held) * size, size), size)
            dest = out_ref.at[slot_ref[s] // held, rows]
            copies.append(pltpu.make_async_copy(tiles_ref.at[s], dest, sems.at[s]))
        dest = out_ref.at[:, pl.ds(held * size, extra)]
        copies.append(pltpu.make_async_copy(notes_ref, dest, sems.at[count]))
        for copy in copies:
            copy.start()
        for copy in copies:
            copy.wait()

    return pl.pallas_call(
        kernel,
        out_shape=jax.ShapeDtypeStruct((peers, held * size + extra, size), tile_data.dtype),
        in_specs=[
            pl.BlockSpec(memory_space=pltpu.SMEM),
            pl.BlockSpec(memory_space=pl.ANY),
            pl.BlockSpec(memory_space=pltpu.VMEM),
        ],
        out_specs=pl.BlockSpec(memory_space=pl.ANY),
        scratch_shapes=[pltpu.SemaphoreType.DMA((count + 1,))],
        compiler_params=params(),
    )(slot, tile_data, notes)


def row_products(inbox, meta, me, pieces, his, los, width):
    senders, size = inbox.shape[0], inbox.shape[2]
    held = meta.shape[1]
    part, length = pieces[0].shape
    rank = 2 * part
    per_chunk = width // size

    def kernel(meta_ref, me_ref, tile_ref, *refs):
        piece_refs, (top_ref, bot_ref), (panel_ref, term_ref) = refs[: 2 * his], refs[-4:-2], refs[-2:]
        step = pl.program_id(0)
        my_core, my_hi, my_lo = me_ref[1], me_ref[2], me_ref[3]

        @pl.when(step == 0)
        def _():
            top_ref[...] = jnp.zeros_like(top_ref)
            bot_ref[...] = jnp.zeros_like(bot_ref)
            for side in range(2):
                rows = pl.ds(pl.multiple_of((my_core ^ side) * part, part), part)
                for j in range(his):
                    panel_ref[j, rows, :] = piece_refs[side * his + j][...]

        for item in range(BATCH * held):
            sub, slot = item // held, item % held
            spot = jnp.maximum(meta_ref[step * BATCH + sub, slot] - 1, 0)
            place = pl.ds(pl.multiple_of((spot % CT) * size, size), size)
            term_ref[item] = lax.dot_general(
                panel_ref[slot // CAP ^ my_hi, :, place],
                tile_ref[sub, slot * size : (slot + 1) * size],
                (((1,), (1,)), ((), ())),
                preferred_element_type=F32,
            )

        for item in range(BATCH * held):
            sub, slot = item // held, item % held
            spot = meta_ref[step * BATCH + sub, slot] - 1

            @pl.when(spot >= 0)
            def _():
                trow = spot // CT
                chunk = trow // per_chunk
                lanes = pl.ds(pl.multiple_of((trow % per_chunk) * size, size), size)
                at = (chunk % los ^ my_lo, chunk // los ^ my_hi)
                top_ref[at[0], at[1], :, lanes] += term_ref[item, :part]
                bot_ref[at[0], at[1], :, lanes] += term_ref[item, part:]

    shape = (los, his, part, width)
    piece_spec = pl.BlockSpec((part, length), lambda i, *_: (0, 0))
    out_spec = pl.BlockSpec(shape, lambda i, *_: (0, 0, 0, 0))
    return pl.pallas_call(
        kernel,
        out_shape=[jax.ShapeDtypeStruct(shape, F32)] * 2,
        grid_spec=pltpu.PrefetchScalarGridSpec(
            num_scalar_prefetch=2,
            grid=(senders // BATCH,),
            in_specs=[pl.BlockSpec((BATCH, inbox.shape[1], size), lambda i, *_: (i, 0, 0))]
            + [piece_spec] * (2 * his),
            out_specs=[out_spec] * 2,
            scratch_shapes=[
                pltpu.VMEM((his, rank, length), jnp.bfloat16),
                pltpu.VMEM((BATCH * held, rank, size), F32),
            ],
        ),
        compiler_params=params(),
    )(meta, me, inbox, *pieces)


def column_products(inbox, meta, me, pieces, his, los, fars, out_width):
    senders, size = inbox.shape[0], inbox.shape[2]
    held = meta.shape[1]
    rank, width = pieces[0].shape
    part = rank // 2
    per_chunk, per_out = width // size, out_width // size
    chunks = his * los

    def kernel(meta_ref, me_ref, tile_ref, *refs):
        piece_refs, outs, gram_ref = refs[:chunks], refs[chunks : chunks + 4], refs[chunks + 4]
        panel_ref, term_ref = refs[-2:]
        keeps, sends = outs[:2], outs[2:]
        step = pl.program_id(0)
        my_far, my_core, my_hi, my_lo = (me_ref[i] for i in range(4))

        @pl.when(step == 0)
        def _():
            for out in outs:
                out[...] = jnp.zeros_like(out)
            gram = jnp.zeros((rank, rank), F32)
            for j in range(chunks):
                piece = piece_refs[j][...]
                panel_ref[j] = piece
                gram += lax.dot_general(
                    piece, piece, (((1,), (1,)), ((), ())), preferred_element_type=F32
                )
            gram_ref[...] = gram

        for item in range(BATCH * held):
            sub, slot = item // held, item % held
            spot = jnp.maximum(meta_ref[step * BATCH + sub, slot] - 1, 0)
            trow = spot // CT
            chunk = trow // per_chunk
            lanes = pl.ds(pl.multiple_of((trow % per_chunk) * size, size), size)
            at = (chunk // los ^ my_hi) * los + (chunk % los ^ my_lo)
            term_ref[item] = lax.dot_general(
                panel_ref[at, :, lanes],
                tile_ref[sub, slot * size : (slot + 1) * size],
                (((1,), (0,)), ((), ())),
                preferred_element_type=F32,
            )

        for item in range(BATCH * held):
            sub, slot = item // held, item % held
            spot = meta_ref[step * BATCH + sub, slot] - 1
            tcol = spot % CT
            owner = tcol // per_out
            place = pl.ds(pl.multiple_of((tcol % per_out) * size, size), size)
            at = (owner // 2 ^ my_far, slot // CAP ^ my_hi)
            for side, dests in enumerate((keeps, sends)):

                @pl.when((spot >= 0) & ((owner ^ my_core) % 2 == side))
                def _():
                    dests[0][at[0], at[1], :, place] += term_ref[item, :part]
                    dests[1][at[0], at[1], :, place] += term_ref[item, part:]

    shape = (fars, his, part, out_width)
    out_spec = pl.BlockSpec(shape, lambda i, *_: (0, 0, 0, 0))
    return pl.pallas_call(
        kernel,
        out_shape=[jax.ShapeDtypeStruct(shape, F32)] * 4
        + [jax.ShapeDtypeStruct((rank, rank), F32)],
        grid_spec=pltpu.PrefetchScalarGridSpec(
            num_scalar_prefetch=2,
            grid=(senders // BATCH,),
            in_specs=[pl.BlockSpec((BATCH, inbox.shape[1], size), lambda i, *_: (i, 0, 0))]
            + [pl.BlockSpec((rank, width), lambda i, *_: (0, 0))] * chunks,
            out_specs=[out_spec] * 4 + [pl.BlockSpec((rank, rank), lambda i, *_: (0, 0))],
            scratch_shapes=[
                pltpu.VMEM((chunks, rank, width), jnp.bfloat16),
                pltpu.VMEM((BATCH * held, rank, size), F32),
            ],
        ),
        compiler_params=params(),
    )(meta, me, inbox, *pieces)


def assemble(pieces, place, turned):
    count = len(pieces)
    rank, width = pieces[0].shape if turned else pieces[0].shape[::-1]

    def kernel(place_ref, *refs):
        for j in range(count):
            piece = refs[j][...].astype(F32)
            refs[count][j ^ place_ref[0]] = jnp.transpose(piece) if turned else piece

    return pl.pallas_call(
        kernel,
        out_shape=jax.ShapeDtypeStruct((count, width, rank), F32),
        in_specs=[pl.BlockSpec(memory_space=pltpu.SMEM)]
        + [pl.BlockSpec(memory_space=pltpu.VMEM)] * count,
        out_specs=pl.BlockSpec(memory_space=pltpu.VMEM),
        compiler_params=params(),
    )(place, *pieces).reshape(count * width, rank)


def prepare(factor, gram):
    rank, width = factor.shape

    def kernel(factor_ref, gram_ref, part_ref, mixed_ref, over_ref):
        gram = gram_ref[...]
        shape = (rank, rank)
        diag = lax.broadcasted_iota(jnp.int32, shape, 0) == lax.broadcasted_iota(jnp.int32, shape, 1)
        over = 1.0 / (jnp.sum(jnp.where(diag, gram, 0.0), axis=1, keepdims=True) + RIDGE)
        mixed = gram * over
        mixed_ref[...] = mixed
        over_ref[...] = jnp.broadcast_to(over, shape)
        part_ref[...] = jnp.dot(
            jnp.where(diag, 0.0, mixed), factor_ref[...], precision=HIGH, preferred_element_type=F32
        )

    return pl.pallas_call(
        kernel,
        out_shape=[
            jax.ShapeDtypeStruct((rank, width), F32),
            jax.ShapeDtypeStruct((rank, rank), F32),
            jax.ShapeDtypeStruct((rank, rank), F32),
        ],
        compiler_params=params(),
    )(factor, gram)


def sweep_block(factor, top, bottom, part, mixed, over):
    rank, half = factor.shape[0], factor.shape[0] // 2
    over = over[:, :1]
    ahead = []
    for lead in range(0, rank, STEP):
        product = top[lead : lead + STEP] if lead < half else bottom[lead - half : lead - half + STEP]
        ahead.append(product * over[lead : lead + STEP] - part[lead : lead + STEP])
    outs = []
    for b in range(rank // STEP):
        here = slice(b * STEP, (b + 1) * STEP)
        before, block, left = factor[here], mixed[here, here], ahead[b]
        news, moves = [], []
        for k in range(STEP):
            new = jnp.maximum(left[k : k + 1], EPS)
            move = new - before[k : k + 1]
            news.append(new)
            moves.append(move)
            if k + 1 < STEP:
                left = left - block[:, k : k + 1] * move
        outs.append(jnp.concatenate(news, axis=0))
        moved = jnp.concatenate(moves, axis=0)
        for c in range(b + 1, rank // STEP):
            ahead[c] -= jnp.dot(
                mixed[c * STEP : (c + 1) * STEP, here], moved, precision=HIGH, preferred_element_type=F32
            )
    return jnp.concatenate(outs, axis=0)


def sweep(factor, top, bottom, prepared, turned):
    rank, width = factor.shape

    def kernel(*refs):
        new = sweep_block(*(ref[...] for ref in refs[:-1]))
        refs[-1][...] = (jnp.transpose(new) if turned else new).astype(jnp.bfloat16)

    shape = (width, rank) if turned else (rank, width)
    return pl.pallas_call(
        kernel, out_shape=jax.ShapeDtypeStruct(shape, jnp.bfloat16), compiler_params=params()
    )(factor, top, bottom, *prepared)


def swap(x, axis, bit):
    size = lax.axis_size(axis)
    return lax.ppermute(x, axis, [(i, i ^ bit) for i in range(size)])


def bits(axis):
    bit = 1
    while bit < lax.axis_size(axis):
        yield bit
        bit *= 2


def everywhere(x, axes, combine):
    for axis in axes:
        for bit in bits(axis):
            x = combine(x, swap(x, axis, bit))
    return x


def spread(pieces, axis):
    return [
        piece if j == 0 else swap(piece, axis, j)
        for piece in pieces
        for j in range(lax.axis_size(axis))
    ]


def pull(total, sums, axis, up, down):
    for j in range(1, lax.axis_size(axis)):
        total = total + swap((sums[j - 1] * up).astype(LINK), axis, j).astype(F32) * down
    return total


def gather(sums, axis, up, down):
    return pull(sums[0], sums[1:], axis, up, down)


def scales(gram, terms, size):
    rank = gram.shape[0]
    norm = jnp.sqrt(jnp.maximum(jnp.sum(gram * jnp.eye(rank, dtype=F32), axis=1, keepdims=True), 1e-24))
    down = norm * (terms * PEAK * size**0.5 / 32768.0)
    half = rank // 2
    return [(1.0 / d, d) for d in (down[:half], down[half:])]


def local(tile_data, owner_ids, tile_spot, w_init, h_init):
    row_axes, col_axes = ("far", "core"), ("hi", "lo")
    fars, cores = lax.axis_size("far"), lax.axis_size("core")
    his, los = lax.axis_size("hi"), lax.axis_size("lo")
    rows, cols = fars * cores, his * los
    slots = rows * cols * CAP
    size, rank = tile_data.shape[1], w_init.shape[1]
    width, length = w_init.shape[0] // cols, h_init.shape[0] // rows
    my_row, my_col = lax.axis_index(row_axes), lax.axis_index(col_axes)
    core = lax.axis_index("core")
    me = jnp.stack([lax.axis_index(a) for a in row_axes + col_axes]).astype(jnp.int32)

    owner = owner_ids[:, 0]
    count = owner.shape[0]
    same = owner[:, None] == owner[None, :]
    earlier = jnp.arange(count)[None, :] < jnp.arange(count)[:, None]
    nth = jnp.sum((same & earlier).astype(jnp.int32), axis=1)
    o_row, o_col = owner // cols, owner % cols
    slot = ((o_row * los + o_col % los) * his + o_col // los) * CAP + nth

    plane = ("far", "core", "lo")
    peers, held = rows * los, his * CAP
    marks = slot[:, None] == jnp.arange(slots, dtype=jnp.int32)[None, :]
    meta = jnp.sum(jnp.where(marks, tile_spot[:, None] + 1, 0), axis=0).reshape(peers, held)
    notes = jnp.broadcast_to(meta.astype(tile_data.dtype)[:, None, :], (peers, 16, held))
    notes = jnp.pad(notes, ((0, 0), (0, 0), (0, size - held)))
    outbox = pack(slot, tile_data, notes, held)
    outbox, h_init = lax.optimization_barrier((outbox, h_init))
    inbox = lax.all_to_all(outbox, plane, split_axis=0, concat_axis=0, tiled=True)
    meta = inbox[:, held * size, :held].astype(F32).astype(jnp.int32)

    h_t = h_init.T
    piece = lax.dynamic_slice_in_dim(h_t, core * (rank // 2), rank // 2, 0).astype(jnp.bfloat16)
    pieces = spread([piece], "hi")
    pieces += [swap(piece, "core", 1) for piece in pieces]

    gram_h = lax.dot_general(h_t, h_t, (((1,), (1,)), ((), ())), precision=HIGH)
    gram_h = everywhere(gram_h, col_axes, jnp.add)
    w_t = lax.dynamic_slice_in_dim(w_init, my_col * width, width, 0).T
    prepared = prepare(w_t, gram_h)
    parts = row_products(inbox, meta, me, pieces, his, los, width)
    sums = []
    for part, scale in zip(parts, scales(gram_h, slots * los, size)):
        sums.append(gather(gather(part, "lo", *scale), "hi", *scale))
    w_low = sweep(w_t, *sums, prepared, False)
    pieces = spread(spread([w_low], "hi"), "lo")

    *parts, gram_w = column_products(inbox, meta, me, pieces, his, los, fars, length)
    gram_w = everywhere(gram_w, row_axes, jnp.add)
    w_new = assemble(pieces, my_col[None].astype(jnp.int32), True)
    own_t = lax.dynamic_slice_in_dim(h_init, my_row * length, length, 0).T
    prepared = prepare(own_t, gram_w)
    sums = []
    for keep, send, scale in zip(parts[:2], parts[2:], scales(gram_w, slots * rows, size)):
        keep = keep + swap(send, "core", 1)
        half = fars // 2
        while half:
            up, down = scale
            away = swap((keep[half:] * up).astype(LINK), "far", half)
            keep = keep[:half] + away.astype(F32) * down
            half //= 2
        sums.append(gather(keep[0], "hi", *scale))
    h_low = sweep(own_t, *sums, prepared, True)
    h_new = assemble(spread(spread([h_low], "far"), "core"), my_row[None].astype(jnp.int32), False)
    return w_new, h_new


def solution(mesh):
    rows, cols = mesh.shape["row"], mesh.shape["col"]
    his = 4 if cols % 4 == 0 else 1
    shape = (rows // 2, 2, his, cols // his)
    fine = Mesh(mesh.devices.reshape(shape), ("far", "core", "hi", "lo"))
    row, col = ("far", "core"), ("hi", "lo")
    in_specs = (P(row + col, None, None), P(row + col, None), P(row + col), P(row, None), P(col, None))
    out_specs = (P(row, None), P(col, None))
    return jax.shard_map(local, mesh=fine, in_specs=in_specs, out_specs=out_specs, check_vma=False)
```

```python
import jax
import jax.numpy as jnp
from jax import lax
from jax.experimental import pallas as pl
from jax.experimental.pallas import tpu as pltpu
from jax.sharding import Mesh
from jax.sharding import PartitionSpec as P

CT = 16
CAP = 2
EPS = 1e-06
RIDGE = 1.0
HIGH = lax.Precision.HIGHEST
F32 = jnp.float32
LINK = jnp.float16
STEP = 32
DEPTH = 8
PEAK = 256.0
CUT = 80
VMEM_LIMIT = 32 * 2**20


def params(limit=VMEM_LIMIT):
    return pltpu.CompilerParams(vmem_limit_bytes=limit)


def pack(owner, spot, tile_data, rows, his, los):
    count, size = tile_data.shape[0], tile_data.shape[1]
    peers, held, extra = rows * los, his * CAP, 16

    def kernel(owner_ref, spot_ref, tiles_ref, out_ref, held_ref, notes_ref, seen_ref, sems):
        ins = [
            pltpu.make_async_copy(tiles_ref.at[s], held_ref.at[s], sems.at[s]) for s in range(count)
        ]
        for copy in ins:
            copy.start()

        def clear(i, carry):
            seen_ref[i] = 0
            return carry

        lax.fori_loop(0, rows * his * los, clear, 0)
        shape = (peers, size)
        peer_of = lax.broadcasted_iota(jnp.int32, shape, 0)
        slot_of = lax.broadcasted_iota(jnp.int32, shape, 1)
        notes = jnp.zeros(shape, F32)
        outs = []
        for s in range(count):
            one = owner_ref[s]
            row, col = one // (his * los), one % (his * los)
            peer, slot = row * los + col % los, col // los * CAP + seen_ref[one]
            seen_ref[one] += 1
            notes = jnp.where((peer_of == peer) & (slot_of == slot), (spot_ref[s] + 1).astype(F32), notes)
            dest = out_ref.at[peer, pl.ds(pl.multiple_of(slot * size, size), size)]
            ins[s].wait()
            outs.append(pltpu.make_async_copy(held_ref.at[s], dest, sems.at[count + s]))
            outs[-1].start()
        for peer in range(peers):
            line = jnp.broadcast_to(notes[peer : peer + 1], (extra, size))
            notes_ref[peer] = line.astype(notes_ref.dtype)
        dest = out_ref.at[:, pl.ds(held * size, extra)]
        outs.append(pltpu.make_async_copy(notes_ref, dest, sems.at[2 * count]))
        outs[-1].start()
        for copy in outs:
            copy.wait()

    smem = pl.BlockSpec(memory_space=pltpu.SMEM)
    return pl.pallas_call(
        kernel,
        out_shape=jax.ShapeDtypeStruct((peers, held * size + extra, size), tile_data.dtype),
        in_specs=[smem, smem, pl.BlockSpec(memory_space=pltpu.HBM)],
        out_specs=pl.BlockSpec(memory_space=pltpu.HBM),
        scratch_shapes=[
            pltpu.VMEM(tile_data.shape, tile_data.dtype),
            pltpu.VMEM((peers, extra, size), tile_data.dtype),
            pltpu.SMEM((rows * his * los,), jnp.int32),
            pltpu.SemaphoreType.DMA((2 * count + 1,)),
        ],
        compiler_params=params(60 * 2**20),
    )(owner, spot, tile_data)


def each_tile(meta_ref, inbox_ref, tiles_ref, terms_ref, sems, product, add, ready):
    held, size, depth = meta_ref.shape[1], terms_ref.shape[2], tiles_ref.shape[0]
    peers = meta_ref.shape[0]

    def copy(peer):
        at = peer % depth
        rows = pl.ds(0, held * size)
        return pltpu.make_async_copy(inbox_ref.at[peer, rows], tiles_ref.at[at], sems.at[at])

    if sems is not None:
        for peer in range(depth):
            copy(peer).start()
    ready()

    def step(peer, carry):
        if sems is not None:
            copy(peer).wait()
        for slot in range(held):
            spot = jnp.maximum(meta_ref[peer, slot] - 1, 0)
            tile = tiles_ref[peer % depth, slot * size : (slot + 1) * size]
            terms_ref[slot] = product(slot, spot, tile)
        for slot in range(held):
            spot = meta_ref[peer, slot] - 1

            @pl.when(spot >= 0)
            def _():
                add(slot, spot)

        if depth < peers:

            @pl.when(peer + depth < peers)
            def _():
                copy(peer + depth).start()

        return carry

    lax.fori_loop(0, peers, step, 0)


def hbm():
    return pl.BlockSpec(memory_space=pltpu.HBM)


def vmem():
    return pl.BlockSpec(memory_space=pltpu.VMEM)


def smem():
    return pl.BlockSpec(memory_space=pltpu.SMEM)


def row_products(inbox, meta, me, pieces, his, los, width):
    peers, size, held = inbox.shape[0], inbox.shape[2], meta.shape[1]
    part, length = pieces[0].shape
    rank = 2 * part
    per_chunk = width // size
    keep = peers <= DEPTH

    def kernel(meta_ref, me_ref, inbox_ref, *refs):
        piece_refs, (top_ref, bot_ref) = refs[: 2 * his], refs[2 * his : 2 * his + 2]
        tiles_ref, panel_ref, terms_ref, sems, more_sems = refs[2 * his + 2 :]
        my_core, my_hi, my_lo = me_ref[1], me_ref[2], me_ref[3]
        copies = []
        for side in range(2):
            rows = pl.ds(pl.multiple_of((my_core ^ side) * part, part), part)
            for j in range(his):
                at = side * his + j
                copies.append(
                    pltpu.make_async_copy(piece_refs[at], panel_ref.at[j, rows], more_sems.at[at])
                )
        for copy in copies:
            copy.start()

        def ready():
            top_ref[...] = jnp.zeros_like(top_ref)
            bot_ref[...] = jnp.zeros_like(bot_ref)
            for copy in copies:
                copy.wait()

        def product(slot, spot, tile):
            place = pl.ds(pl.multiple_of((spot % CT) * size, size), size)
            panel = panel_ref[slot // CAP ^ my_hi, :, place]
            return lax.dot_general(panel, tile, (((1,), (1,)), ((), ())), preferred_element_type=F32)

        def add(slot, spot):
            trow = spot // CT
            chunk = trow // per_chunk
            lanes = pl.ds(pl.multiple_of((trow % per_chunk) * size, size), size)
            hi, lo = chunk // los ^ my_hi, chunk % los ^ my_lo
            top_ref[lo, hi, :, lanes] += terms_ref[slot, :CUT]
            bot_ref[hi, lo, :, lanes] += terms_ref[slot, CUT:]

        each_tile(meta_ref, inbox_ref, tiles_ref, terms_ref, sems, product, add, ready)

    out_shape = [
        jax.ShapeDtypeStruct((los, his, CUT, width), F32),
        jax.ShapeDtypeStruct((his, los, rank - CUT, width), F32),
    ]
    tiles = (min(peers, DEPTH), held * size, size)
    out_tiles = [jax.ShapeDtypeStruct(tiles, inbox.dtype)] if keep else []
    return pl.pallas_call(
        kernel,
        out_shape=out_shape + out_tiles,
        in_specs=[smem(), smem(), hbm()] + [hbm()] * len(pieces),
        out_specs=[vmem()] * (2 + keep),
        scratch_shapes=([] if keep else [pltpu.VMEM(tiles, inbox.dtype)])
        + [
            pltpu.VMEM((his, rank, length), jnp.bfloat16),
            pltpu.VMEM((held, rank, size), F32),
            pltpu.SemaphoreType.DMA((tiles[0],)),
            pltpu.SemaphoreType.DMA((2 * his,)),
        ],
        compiler_params=params(),
    )(meta, me, inbox, *pieces)


def column_products(inbox, kept, meta, me, pieces, his, los, fars, out_width):
    peers, size, held = inbox.shape[0], inbox.shape[2], meta.shape[1]
    rank, width = pieces[0].shape
    per_chunk, per_out = width // size, out_width // size
    chunks = his * los

    def kernel(meta_ref, me_ref, source_ref, *refs):
        piece_refs, outs, gram_ref = refs[:chunks], refs[chunks : chunks + 4], refs[chunks + 4]
        panel_ref, terms_ref, *rest = refs[chunks + 5 :]
        tiles_ref, sems = (source_ref, None) if kept else rest
        my_far, my_core, my_hi, my_lo = (me_ref[i] for i in range(4))

        def ready():
            for out in outs:
                out[...] = jnp.zeros_like(out)
            gram = jnp.zeros((rank, rank), F32)
            for j in range(chunks):
                piece = piece_refs[j][...]
                panel_ref[j] = piece
                gram += lax.dot_general(
                    piece, piece, (((1,), (1,)), ((), ())), preferred_element_type=F32
                )
            gram_ref[...] = gram

        def product(slot, spot, tile):
            trow = spot // CT
            chunk = trow // per_chunk
            lanes = pl.ds(pl.multiple_of((trow % per_chunk) * size, size), size)
            panel = panel_ref[(chunk // los ^ my_hi) * los + (chunk % los ^ my_lo), :, lanes]
            return lax.dot_general(panel, tile, (((1,), (0,)), ((), ())), preferred_element_type=F32)

        def add(slot, spot):
            tcol = spot % CT
            owner = tcol // per_out
            place = pl.ds(pl.multiple_of((tcol % per_out) * size, size), size)
            far, hi = owner // 2 ^ my_far, slot // CAP ^ my_hi
            for side, (top_ref, bot_ref) in enumerate((outs[:2], outs[2:])):

                @pl.when((owner ^ my_core) % 2 == side)
                def _():
                    top_ref[far, hi, :, place] += terms_ref[slot, :CUT]
                    bot_ref[hi, far, :, place] += terms_ref[slot, CUT:]

        each_tile(meta_ref, source_ref, tiles_ref, terms_ref, sems, product, add, ready)

    tops, bots = (fars, his, CUT, out_width), (his, fars, rank - CUT, out_width)
    out_shape = [tops, bots, tops, bots, (rank, rank)]
    scratch = [
        pltpu.VMEM((chunks, rank, width), jnp.bfloat16),
        pltpu.VMEM((held, rank, size), F32),
    ]
    if not kept:
        scratch.append(pltpu.VMEM((DEPTH, held * size, size), inbox.dtype))
        scratch.append(pltpu.SemaphoreType.DMA((DEPTH,)))
    return pl.pallas_call(
        kernel,
        out_shape=[jax.ShapeDtypeStruct(shape, F32) for shape in out_shape],
        in_specs=[smem(), smem(), vmem() if kept else hbm()] + [vmem()] * chunks,
        out_specs=[vmem()] * len(out_shape),
        scratch_shapes=scratch,
        compiler_params=params(),
    )(meta, me, *(kept or [inbox]), *pieces)


def assemble(pieces, place, turned):
    count = len(pieces)
    rank, width = pieces[0].shape if turned else pieces[0].shape[::-1]

    def kernel(place_ref, *refs):
        for j in range(count):
            piece = refs[j][...].astype(F32)
            refs[count][j ^ place_ref[0]] = jnp.transpose(piece) if turned else piece

    return pl.pallas_call(
        kernel,
        out_shape=jax.ShapeDtypeStruct((count, width, rank), F32),
        in_specs=[pl.BlockSpec(memory_space=pltpu.SMEM)]
        + [pl.BlockSpec(memory_space=pltpu.VMEM)] * count,
        out_specs=pl.BlockSpec(memory_space=pltpu.VMEM),
        compiler_params=params(),
    )(place, *pieces).reshape(count * width, rank)


def prepare(factor, gram):
    rank, width = factor.shape

    def kernel(factor_ref, gram_ref, part_ref, mixed_ref, over_ref):
        gram = gram_ref[...]
        shape = (rank, rank)
        diag = lax.broadcasted_iota(jnp.int32, shape, 0) == lax.broadcasted_iota(jnp.int32, shape, 1)
        over = 1.0 / (jnp.sum(jnp.where(diag, gram, 0.0), axis=1, keepdims=True) + RIDGE)
        mixed = gram * over
        mixed_ref[...] = mixed
        over_ref[...] = jnp.broadcast_to(over, shape)
        part_ref[...] = jnp.dot(
            jnp.where(diag, 0.0, mixed), factor_ref[...], precision=HIGH, preferred_element_type=F32
        )

    return pl.pallas_call(
        kernel,
        out_shape=[
            jax.ShapeDtypeStruct((rank, width), F32),
            jax.ShapeDtypeStruct((rank, rank), F32),
            jax.ShapeDtypeStruct((rank, rank), F32),
        ],
        compiler_params=params(),
    )(factor, gram)


def sweep_block(factor, top, bottom, part, mixed, over):
    rank = factor.shape[0]
    product = jnp.concatenate([top, bottom], axis=0)
    over = over[:, :1]
    ahead = []
    for lead in range(0, rank, STEP):
        here = slice(lead, lead + STEP)
        ahead.append(product[here] * over[here] - part[here])
    outs = []
    for b in range(rank // STEP):
        here = slice(b * STEP, (b + 1) * STEP)
        before, block, left = factor[here], mixed[here, here], ahead[b]
        news, moves = [], []
        for k in range(STEP):
            new = jnp.maximum(left[k : k + 1], EPS)
            move = new - before[k : k + 1]
            news.append(new)
            moves.append(move)
            if k + 1 < STEP:
                left = left - block[:, k : k + 1] * move
        outs.append(jnp.concatenate(news, axis=0))
        moved = jnp.concatenate(moves, axis=0)
        for c in range(b + 1, rank // STEP):
            ahead[c] -= jnp.dot(
                mixed[c * STEP : (c + 1) * STEP, here], moved, precision=HIGH, preferred_element_type=F32
            )
    return jnp.concatenate(outs, axis=0)


def sweep(factor, top, bottom, prepared, turned):
    rank, width = factor.shape

    def kernel(*refs):
        new = sweep_block(*(ref[...] for ref in refs[:-1]))
        refs[-1][...] = (jnp.transpose(new) if turned else new).astype(jnp.bfloat16)

    shape = (width, rank) if turned else (rank, width)
    return pl.pallas_call(
        kernel, out_shape=jax.ShapeDtypeStruct(shape, jnp.bfloat16), compiler_params=params()
    )(factor, top, bottom, *prepared)


def swap(x, axis, bit):
    size = lax.axis_size(axis)
    return lax.ppermute(x, axis, [(i, i ^ bit) for i in range(size)])


def bits(axis):
    bit = 1
    while bit < lax.axis_size(axis):
        yield bit
        bit *= 2


def everywhere(x, axes, combine):
    for axis in axes:
        for bit in bits(axis):
            x = combine(x, swap(x, axis, bit))
    return x


def spread(pieces, axis):
    return [
        piece if j == 0 else swap(piece, axis, j)
        for piece in pieces
        for j in range(lax.axis_size(axis))
    ]


def gather(sums, axis, up, down):
    total = sums[0]
    for j in range(1, lax.axis_size(axis)):
        total = total + swap((sums[j] * up).astype(LINK), axis, j).astype(F32) * down
    return total


def scales(gram, terms, size):
    rank = gram.shape[0]
    norm = jnp.sqrt(jnp.maximum(jnp.sum(gram * jnp.eye(rank, dtype=F32), axis=1, keepdims=True), 1e-24))
    down = norm * (terms * PEAK * size**0.5 / 32768.0)
    return [(1.0 / d, d) for d in (down[:CUT], down[CUT:])]


def local(tile_data, owner_ids, tile_spot, w_init, h_init):
    row_axes, col_axes = ("far", "core"), ("hi", "lo")
    fars, cores = lax.axis_size("far"), lax.axis_size("core")
    his, los = lax.axis_size("hi"), lax.axis_size("lo")
    rows, cols = fars * cores, his * los
    slots = rows * cols * CAP
    size, rank = tile_data.shape[1], w_init.shape[1]
    width, length = w_init.shape[0] // cols, h_init.shape[0] // rows
    my_row, my_col = lax.axis_index(row_axes), lax.axis_index(col_axes)
    core = lax.axis_index("core")
    me = jnp.stack([lax.axis_index(a) for a in row_axes + col_axes]).astype(jnp.int32)

    plane = ("far", "core", "lo")
    held = his * CAP
    outbox = pack(owner_ids[:, 0], tile_spot, tile_data, rows, his, los)
    outbox, h_init = lax.optimization_barrier((outbox, h_init))
    inbox = lax.all_to_all(outbox, plane, split_axis=0, concat_axis=0, tiled=True)
    meta = inbox[:, held * size, :held].astype(F32).astype(jnp.int32)

    h_t = h_init.T
    piece = lax.dynamic_slice_in_dim(h_t, core * (rank // 2), rank // 2, 0).astype(jnp.bfloat16)
    pieces = spread([piece], "hi")
    pieces += [swap(piece, "core", 1) for piece in pieces]

    gram_h = lax.dot_general(h_t, h_t, (((1,), (1,)), ((), ())), precision=HIGH)
    gram_h = everywhere(gram_h, col_axes, jnp.add)
    w_t = lax.dynamic_slice_in_dim(w_init, my_col * width, width, 0).T
    prepared = prepare(w_t, gram_h)
    parts = row_products(inbox, meta, me, pieces, his, los, width)
    parts, kept = parts[:2], parts[2:]
    high, low = scales(gram_h, slots * cols, size)
    top = gather(gather(parts[0], "lo", *high), "hi", *high)
    bottom = gather(gather(parts[1], "hi", *low), "lo", *low)
    w_low = sweep(w_t, top, bottom, prepared, False)
    pieces = spread(spread([w_low], "hi"), "lo")

    *parts, gram_w = column_products(inbox, kept, meta, me, pieces, his, los, fars, length)
    gram_w = everywhere(gram_w, row_axes, jnp.add)
    w_new = assemble(pieces, my_col[None].astype(jnp.int32), True)
    own_t = lax.dynamic_slice_in_dim(h_init, my_row * length, length, 0).T
    prepared = prepare(own_t, gram_w)
    high, low = scales(gram_w, slots * rows * his, size)
    bottom = parts[1] + swap(parts[3], "core", 1)
    top = parts[0] + swap(parts[2], "core", 1)
    bottom = gather(gather(bottom, "hi", *low), "far", *low)
    top = gather(top, "far", *high)
    top, w_new = lax.optimization_barrier((top, w_new))
    top = gather(top, "hi", *high)
    h_low = sweep(own_t, top, bottom, prepared, True)
    h_new = assemble(spread(spread([h_low], "far"), "core"), my_row[None].astype(jnp.int32), False)
    return w_new, h_new


def solution(mesh):
    rows, cols = mesh.shape["row"], mesh.shape["col"]
    his = 4 if cols % 4 == 0 else 1
    shape = (rows // 2, 2, his, cols // his)
    fine = Mesh(mesh.devices.reshape(shape), ("far", "core", "hi", "lo"))
    row, col = ("far", "core"), ("hi", "lo")
    in_specs = (P(row + col, None, None), P(row + col, None), P(row + col), P(row, None), P(col, None))
    out_specs = (P(row, None), P(col, None))
    return jax.shard_map(local, mesh=fine, in_specs=in_specs, out_specs=out_specs, check_vma=False)
```

```python
import jax
import jax.numpy as jnp
from jax import lax
from jax.experimental import pallas as pl
from jax.experimental.pallas import tpu as pltpu
from jax.sharding import Mesh
from jax.sharding import PartitionSpec as P

CT = 16
CAP = 2
EPS = 1e-06
RIDGE = 1.0
HIGH = lax.Precision.HIGHEST
F32 = jnp.float32
LINK = jnp.float16
STEP = 32
DEPTH = 8
PEAK = 256.0
CUT = 80
VMEM_LIMIT = 24 * 2**20


def params(limit=VMEM_LIMIT):
    return pltpu.CompilerParams(vmem_limit_bytes=limit)


def pack(owner, spot, tile_data, rows, his, los):
    count, size = tile_data.shape[0], tile_data.shape[1]
    peers, held, extra = rows * los, his * CAP, 16

    def kernel(owner_ref, spot_ref, tiles_ref, out_ref, held_ref, notes_ref, seen_ref, sems):
        ins = [
            pltpu.make_async_copy(tiles_ref.at[s], held_ref.at[s], sems.at[s]) for s in range(count)
        ]
        for copy in ins:
            copy.start()

        def clear(i, carry):
            seen_ref[i] = 0
            return carry

        lax.fori_loop(0, rows * his * los, clear, 0)
        shape = (peers, size)
        peer_of = lax.broadcasted_iota(jnp.int32, shape, 0)
        slot_of = lax.broadcasted_iota(jnp.int32, shape, 1)
        notes = jnp.zeros(shape, F32)
        outs = []
        for s in range(count):
            one = owner_ref[s]
            row, col = one // (his * los), one % (his * los)
            peer, slot = row * los + col % los, col // los * CAP + seen_ref[one]
            seen_ref[one] += 1
            notes = jnp.where((peer_of == peer) & (slot_of == slot), (spot_ref[s] + 1).astype(F32), notes)
            dest = out_ref.at[peer, pl.ds(pl.multiple_of(slot * size, size), size)]
            ins[s].wait()
            outs.append(pltpu.make_async_copy(held_ref.at[s], dest, sems.at[count + s]))
            outs[-1].start()
        for peer in range(peers):
            line = jnp.broadcast_to(notes[peer : peer + 1], (extra, size))
            notes_ref[peer] = line.astype(notes_ref.dtype)
        dest = out_ref.at[:, pl.ds(held * size, extra)]
        outs.append(pltpu.make_async_copy(notes_ref, dest, sems.at[2 * count]))
        outs[-1].start()
        for copy in outs:
            copy.wait()

    smem = pl.BlockSpec(memory_space=pltpu.SMEM)
    return pl.pallas_call(
        kernel,
        out_shape=jax.ShapeDtypeStruct((peers, held * size + extra, size), tile_data.dtype),
        in_specs=[smem, smem, pl.BlockSpec(memory_space=pltpu.HBM)],
        out_specs=pl.BlockSpec(memory_space=pltpu.HBM),
        scratch_shapes=[
            pltpu.VMEM(tile_data.shape, tile_data.dtype),
            pltpu.VMEM((peers, extra, size), tile_data.dtype),
            pltpu.SMEM((rows * his * los,), jnp.int32),
            pltpu.SemaphoreType.DMA((2 * count + 1,)),
        ],
        compiler_params=params(60 * 2**20),
    )(owner, spot, tile_data)


def each_tile(meta_ref, inbox_ref, tiles_ref, terms_ref, sems, product, add, ready):
    held, size, depth = meta_ref.shape[1], terms_ref.shape[2], tiles_ref.shape[0]
    peers = meta_ref.shape[0]

    def copy(peer):
        at = peer % depth
        rows = pl.ds(0, held * size)
        return pltpu.make_async_copy(inbox_ref.at[peer, rows], tiles_ref.at[at], sems.at[at])

    if sems is not None:
        for peer in range(depth):
            copy(peer).start()
    ready()

    def step(peer, carry):
        if sems is not None:
            copy(peer).wait()
        for slot in range(held):
            spot = jnp.maximum(meta_ref[peer, slot] - 1, 0)
            tile = tiles_ref[peer % depth, slot * size : (slot + 1) * size]
            terms_ref[slot] = product(slot, spot, tile)
        for slot in range(held):
            spot = meta_ref[peer, slot] - 1

            @pl.when(spot >= 0)
            def _():
                add(slot, spot)

        if depth < peers:

            @pl.when(peer + depth < peers)
            def _():
                copy(peer + depth).start()

        return carry

    lax.fori_loop(0, peers, step, 0)


def hbm():
    return pl.BlockSpec(memory_space=pltpu.HBM)


def vmem():
    return pl.BlockSpec(memory_space=pltpu.VMEM)


def smem():
    return pl.BlockSpec(memory_space=pltpu.SMEM)


def row_products(inbox, meta, me, pieces, his, los, width):
    peers, size, held = inbox.shape[0], inbox.shape[2], meta.shape[1]
    part, length = pieces[0].shape
    rank = 2 * part
    per_chunk = width // size
    keep = peers <= DEPTH

    def kernel(meta_ref, me_ref, inbox_ref, *refs):
        piece_refs, (top_ref, bot_ref) = refs[: 2 * his], refs[2 * his : 2 * his + 2]
        tiles_ref, panel_ref, terms_ref, sems, more_sems = refs[2 * his + 2 :]
        my_core, my_hi, my_lo = me_ref[1], me_ref[2], me_ref[3]
        copies = []
        for side in range(2):
            rows = pl.ds(pl.multiple_of((my_core ^ side) * part, part), part)
            for j in range(his):
                at = side * his + j
                copies.append(
                    pltpu.make_async_copy(piece_refs[at], panel_ref.at[j, rows], more_sems.at[at])
                )
        for copy in copies:
            copy.start()

        def ready():
            top_ref[...] = jnp.zeros_like(top_ref)
            bot_ref[...] = jnp.zeros_like(bot_ref)
            for copy in copies:
                copy.wait()

        def product(slot, spot, tile):
            place = pl.ds(pl.multiple_of((spot % CT) * size, size), size)
            panel = panel_ref[slot // CAP ^ my_hi, :, place]
            return lax.dot_general(panel, tile, (((1,), (1,)), ((), ())), preferred_element_type=F32)

        def add(slot, spot):
            trow = spot // CT
            chunk = trow // per_chunk
            lanes = pl.ds(pl.multiple_of((trow % per_chunk) * size, size), size)
            hi, lo = chunk // los ^ my_hi, chunk % los ^ my_lo
            top_ref[lo, hi, :, lanes] += terms_ref[slot, :CUT]
            bot_ref[hi, lo, :, lanes] += terms_ref[slot, CUT:]

        each_tile(meta_ref, inbox_ref, tiles_ref, terms_ref, sems, product, add, ready)

    out_shape = [
        jax.ShapeDtypeStruct((los, his, CUT, width), F32),
        jax.ShapeDtypeStruct((his, los, rank - CUT, width), F32),
    ]
    tiles = (min(peers, DEPTH), held * size, size)
    out_tiles = [jax.ShapeDtypeStruct(tiles, inbox.dtype)] if keep else []
    return pl.pallas_call(
        kernel,
        out_shape=out_shape + out_tiles,
        in_specs=[smem(), smem(), hbm()] + [vmem()] * len(pieces),
        out_specs=[vmem()] * (2 + keep),
        scratch_shapes=([] if keep else [pltpu.VMEM(tiles, inbox.dtype)])
        + [
            pltpu.VMEM((his, rank, length), jnp.bfloat16),
            pltpu.VMEM((held, rank, size), F32),
            pltpu.SemaphoreType.DMA((tiles[0],)),
            pltpu.SemaphoreType.DMA((2 * his,)),
        ],
        compiler_params=params(),
    )(meta, me, inbox, *pieces)


def column_products(inbox, kept, meta, me, pieces, his, los, fars, out_width):
    peers, size, held = inbox.shape[0], inbox.shape[2], meta.shape[1]
    rank, width = pieces[0].shape
    per_chunk, per_out = width // size, out_width // size
    chunks = his * los

    def kernel(meta_ref, me_ref, source_ref, *refs):
        piece_refs, outs = refs[:chunks], refs[chunks : chunks + 4]
        panel_ref, terms_ref, *rest = refs[chunks + 4 :]
        tiles_ref, sems = (source_ref, None) if kept else rest
        my_far, my_core, my_hi, my_lo = (me_ref[i] for i in range(4))

        def ready():
            for out in outs:
                out[...] = jnp.zeros_like(out)
            gram = jnp.zeros((rank, rank), F32)
            for j in range(chunks):
                piece = piece_refs[j][...]
                panel_ref[j] = piece
                gram += lax.dot_general(
                    piece, piece, (((1,), (1,)), ((), ())), preferred_element_type=F32
                )
            shape = (rank, rank)
            diag = lax.broadcasted_iota(jnp.int32, shape, 0) == lax.broadcasted_iota(jnp.int32, shape, 1)
            norms = jnp.sum(jnp.where(diag, gram, 0.0), axis=1, keepdims=True)[CUT:]
            lines = rank * rank // out_width
            for out in (outs[1], outs[3]):
                out[his * fars] = jnp.broadcast_to(norms, out.shape[1:])
                for j in range(rank // lines):
                    out[his * fars + 1, :lines, j * rank : (j + 1) * rank] = gram[j * lines : (j + 1) * lines]

        def product(slot, spot, tile):
            trow = spot // CT
            chunk = trow // per_chunk
            lanes = pl.ds(pl.multiple_of((trow % per_chunk) * size, size), size)
            panel = panel_ref[(chunk // los ^ my_hi) * los + (chunk % los ^ my_lo), :, lanes]
            return lax.dot_general(panel, tile, (((1,), (0,)), ((), ())), preferred_element_type=F32)

        def add(slot, spot):
            tcol = spot % CT
            owner = tcol // per_out
            place = pl.ds(pl.multiple_of((tcol % per_out) * size, size), size)
            far, hi = owner // 2 ^ my_far, slot // CAP ^ my_hi
            for side, (top_ref, bot_ref) in enumerate((outs[:2], outs[2:])):

                @pl.when((owner ^ my_core) % 2 == side)
                def _():
                    top_ref[far, hi, :, place] += terms_ref[slot, :CUT]
                    bot_ref[hi * fars + far, :, place] += terms_ref[slot, CUT:]

        each_tile(meta_ref, source_ref, tiles_ref, terms_ref, sems, product, add, ready)

    tops, bots = (fars, his, CUT, out_width), (his * fars + 2, rank - CUT, out_width)
    out_shape = [tops, bots, tops, bots]
    scratch = [
        pltpu.VMEM((chunks, rank, width), jnp.bfloat16),
        pltpu.VMEM((held, rank, size), F32),
    ]
    if not kept:
        scratch.append(pltpu.VMEM((DEPTH, held * size, size), inbox.dtype))
        scratch.append(pltpu.SemaphoreType.DMA((DEPTH,)))
    return pl.pallas_call(
        kernel,
        out_shape=[jax.ShapeDtypeStruct(shape, F32) for shape in out_shape],
        in_specs=[smem(), smem(), vmem() if kept else hbm()] + [vmem()] * chunks,
        out_specs=[vmem()] * len(out_shape),
        scratch_shapes=scratch,
        compiler_params=params(),
    )(meta, me, *(kept or [inbox]), *pieces)


def assemble(pieces, place, turned):
    count = len(pieces)
    rank, width = pieces[0].shape if turned else pieces[0].shape[::-1]

    def kernel(place_ref, *refs):
        for j in range(count):
            piece = refs[j][...].astype(F32)
            refs[-1][j ^ place_ref[0]] = jnp.transpose(piece) if turned else piece

    return pl.pallas_call(
        kernel,
        out_shape=jax.ShapeDtypeStruct((count, width, rank), F32),
        in_specs=[pl.BlockSpec(memory_space=pltpu.SMEM)]
        + [pl.BlockSpec(memory_space=pltpu.VMEM)] * count,
        out_specs=pl.BlockSpec(memory_space=pltpu.VMEM),
        compiler_params=params(),
    )(place, *pieces).reshape(count * width, rank)


def prepare(factor, gram):
    rank, width = factor.shape

    def kernel(factor_ref, gram_ref, part_ref, mixed_ref, over_ref):
        gram = gram_ref[...]
        shape = (rank, rank)
        diag = lax.broadcasted_iota(jnp.int32, shape, 0) == lax.broadcasted_iota(jnp.int32, shape, 1)
        over = 1.0 / (jnp.sum(jnp.where(diag, gram, 0.0), axis=1, keepdims=True) + RIDGE)
        mixed = gram * over
        mixed_ref[...] = mixed
        over_ref[...] = jnp.broadcast_to(over, shape)
        part_ref[...] = jnp.dot(
            jnp.where(diag, 0.0, mixed), factor_ref[...], precision=HIGH, preferred_element_type=F32
        )

    return pl.pallas_call(
        kernel,
        out_shape=[
            jax.ShapeDtypeStruct((rank, width), F32),
            jax.ShapeDtypeStruct((rank, rank), F32),
            jax.ShapeDtypeStruct((rank, rank), F32),
        ],
        compiler_params=params(),
    )(factor, gram)


def sweep_block(factor, top, bottom, part, mixed, over):
    rank = factor.shape[0]
    product = jnp.concatenate([top, bottom], axis=0)
    over = over[:, :1]
    ahead = []
    for lead in range(0, rank, STEP):
        here = slice(lead, lead + STEP)
        ahead.append(product[here] * over[here] - part[here])
    outs = []
    for b in range(rank // STEP):
        here = slice(b * STEP, (b + 1) * STEP)
        before, block, left = factor[here], mixed[here, here], ahead[b]
        news, moves = [], []
        for k in range(STEP):
            new = jnp.maximum(left[k : k + 1], EPS)
            move = new - before[k : k + 1]
            news.append(new)
            moves.append(move)
            if k + 1 < STEP:
                left = left - block[:, k : k + 1] * move
        outs.append(jnp.concatenate(news, axis=0))
        moved = jnp.concatenate(moves, axis=0)
        for c in range(b + 1, rank // STEP):
            ahead[c] -= jnp.dot(
                mixed[c * STEP : (c + 1) * STEP, here], moved, precision=HIGH, preferred_element_type=F32
            )
    return jnp.concatenate(outs, axis=0)


def sweep(factor, top, bottom, prepared, turned):
    rank, width = factor.shape

    def kernel(*refs):
        new = sweep_block(*(ref[...] for ref in refs[:-1]))
        refs[-1][...] = (jnp.transpose(new) if turned else new).astype(jnp.bfloat16)

    shape = (width, rank) if turned else (rank, width)
    return pl.pallas_call(
        kernel, out_shape=jax.ShapeDtypeStruct(shape, jnp.bfloat16), compiler_params=params()
    )(factor, top, bottom, *prepared)


def swap(x, axis, bit):
    size = lax.axis_size(axis)
    return lax.ppermute(x, axis, [(i, i ^ bit) for i in range(size)])


def bits(axis):
    bit = 1
    while bit < lax.axis_size(axis):
        yield bit
        bit *= 2


def everywhere(x, axes, combine):
    for axis in axes:
        for bit in bits(axis):
            x = combine(x, swap(x, axis, bit))
    return x


def spread(pieces, axis):
    return [
        piece if j == 0 else swap(piece, axis, j)
        for piece in pieces
        for j in range(lax.axis_size(axis))
    ]


def gather(sums, axis, up, down):
    total = sums[0]
    for j in range(1, lax.axis_size(axis)):
        total = total + swap((sums[j] * up).astype(LINK), axis, j).astype(F32) * down
    return total


def bound(squares, terms, size):
    return jnp.sqrt(jnp.maximum(squares, 1e-24)) * (terms * PEAK * size**0.5 / 32768.0)


def scales(gram, terms, size):
    rank = gram.shape[0]
    down = bound(jnp.sum(gram * jnp.eye(rank, dtype=F32), axis=1, keepdims=True), terms, size)
    return [(1.0 / d, d) for d in (down[:CUT], down[CUT:])]


def local(tile_data, owner_ids, tile_spot, w_init, h_init):
    row_axes, col_axes = ("far", "core"), ("hi", "lo")
    fars, cores = lax.axis_size("far"), lax.axis_size("core")
    his, los = lax.axis_size("hi"), lax.axis_size("lo")
    rows, cols = fars * cores, his * los
    slots = rows * cols * CAP
    size, rank = tile_data.shape[1], w_init.shape[1]
    width, length = w_init.shape[0] // cols, h_init.shape[0] // rows
    my_row, my_col = lax.axis_index(row_axes), lax.axis_index(col_axes)
    core = lax.axis_index("core")
    me = jnp.stack([lax.axis_index(a) for a in row_axes + col_axes]).astype(jnp.int32)

    plane = ("far", "core", "lo")
    held = his * CAP
    outbox = pack(owner_ids[:, 0], tile_spot, tile_data, rows, his, los)
    outbox, h_init = lax.optimization_barrier((outbox, h_init))
    inbox = lax.all_to_all(outbox, plane, split_axis=0, concat_axis=0, tiled=True)
    meta = inbox[:, held * size, :held].astype(F32).astype(jnp.int32)

    h_t = h_init.T
    piece = lax.dynamic_slice_in_dim(h_t, core * (rank // 2), rank // 2, 0).astype(jnp.bfloat16)
    pieces = spread([piece], "hi")
    w_t = lax.dynamic_slice_in_dim(w_init, my_col * width, width, 0).T
    own_t = lax.dynamic_slice_in_dim(h_init, my_row * length, length, 0).T
    w_t, own_t, *pieces = lax.optimization_barrier((w_t, own_t, *pieces))
    pieces += [swap(piece, "core", 1) for piece in pieces]

    gram_h = lax.dot_general(h_t, h_t, (((1,), (1,)), ((), ())), precision=HIGH)
    gram_h = everywhere(gram_h, ("hi",), jnp.add)
    gram_h, meta, *pieces = lax.optimization_barrier((gram_h, meta, *pieces))
    gram_h = everywhere(gram_h, ("lo",), jnp.add)
    prepared = prepare(w_t, gram_h)
    parts = row_products(inbox, meta, me, pieces, his, los, width)
    parts, kept = parts[:2], parts[2:]
    high, low = scales(gram_h, slots * cols, size)
    top = gather(gather(parts[0], "lo", *high), "hi", *high)
    bottom = gather(gather(parts[1], "hi", *low), "lo", *low)
    w_low = sweep(w_t, top, bottom, prepared, False)
    pieces = spread(spread([w_low], "hi"), "lo")

    parts = column_products(inbox, kept, meta, me, pieces, his, los, fars, length)

    bottom = parts[1] + swap(parts[3], "core", 1)
    bottom, away = lax.optimization_barrier((bottom, parts[2]))
    top = parts[0] + swap(away, "core", 1)
    lines = rank * rank // length
    gram_w = bottom[-1, :lines].reshape(lines, length // rank, rank)
    gram_w = gram_w.transpose(1, 0, 2).reshape(rank, rank)
    gram_w = everywhere(gram_w, ("far",), jnp.add)
    prepared = prepare(own_t, gram_w)
    high, low = scales(gram_w, slots * rows * his, size)
    down = bound(bottom[-2], slots * 2, size)
    bottom = bottom[:-2].reshape(his, fars, *bottom.shape[1:])
    bottom = gather(bottom, "hi", 1.0 / down, down)
    bottom = gather(bottom, "far", *low)
    top = gather(gather(top, "far", *high), "hi", *high)
    h_low = sweep(own_t, top, bottom, prepared, True)
    h_low, *pieces = lax.optimization_barrier((h_low, *pieces))
    w_new = assemble(pieces, my_col[None].astype(jnp.int32), True)
    pieces = spread([h_low], "far")
    pieces[0], w_new = lax.optimization_barrier((pieces[0], w_new))
    h_new = assemble(spread(pieces, "core"), my_row[None].astype(jnp.int32), False)
    return w_new, h_new


def solution(mesh):
    rows, cols = mesh.shape["row"], mesh.shape["col"]
    his = 4 if cols % 4 == 0 else 1
    shape = (rows // 2, 2, his, cols // his)
    fine = Mesh(mesh.devices.reshape(shape), ("far", "core", "hi", "lo"))
    row, col = ("far", "core"), ("hi", "lo")
    in_specs = (P(row + col, None, None), P(row + col, None), P(row + col), P(row, None), P(col, None))
    out_specs = (P(row, None), P(col, None))
    return jax.shard_map(local, mesh=fine, in_specs=in_specs, out_specs=out_specs, check_vma=False)
```

```python
import jax
import jax.numpy as jnp
from jax import lax
from jax.experimental import pallas as pl
from jax.experimental.pallas import tpu as pltpu
from jax.sharding import Mesh
from jax.sharding import PartitionSpec as P

CT = 16
CAP = 2
EPS = 1e-06
RIDGE = 1.0
HIGH = lax.Precision.HIGHEST
F32 = jnp.float32
LINK = jnp.float16
STEP = 32
DEPTH = 8
PEAK = 256.0
CUT = 80
VMEM_LIMIT = 24 * 2**20


def params(limit=VMEM_LIMIT):
    return pltpu.CompilerParams(vmem_limit_bytes=limit)


def pack(owner, spot, tile_data, rows, his, los):
    count, size = tile_data.shape[0], tile_data.shape[1]
    peers, held, extra = rows * los, his * CAP, 16

    def kernel(owner_ref, spot_ref, tiles_ref, out_ref, held_ref, notes_ref, seen_ref, sems):
        ins = [
            pltpu.make_async_copy(tiles_ref.at[s], held_ref.at[s], sems.at[s]) for s in range(count)
        ]
        for copy in ins:
            copy.start()

        def clear(i, carry):
            seen_ref[i] = 0
            return carry

        lax.fori_loop(0, rows * his * los, clear, 0)
        shape = (peers, size)
        peer_of = lax.broadcasted_iota(jnp.int32, shape, 0)
        slot_of = lax.broadcasted_iota(jnp.int32, shape, 1)
        notes = jnp.zeros(shape, F32)
        outs = []
        for s in range(count):
            one = owner_ref[s]
            row, col = one // (his * los), one % (his * los)
            peer, slot = row * los + col % los, col // los * CAP + seen_ref[one]
            seen_ref[one] += 1
            notes = jnp.where((peer_of == peer) & (slot_of == slot), (spot_ref[s] + 1).astype(F32), notes)
            dest = out_ref.at[peer, pl.ds(pl.multiple_of(slot * size, size), size)]
            ins[s].wait()
            outs.append(pltpu.make_async_copy(held_ref.at[s], dest, sems.at[count + s]))
            outs[-1].start()
        for peer in range(peers):
            line = jnp.broadcast_to(notes[peer : peer + 1], (extra, size))
            notes_ref[peer] = line.astype(notes_ref.dtype)
        dest = out_ref.at[:, pl.ds(held * size, extra)]
        outs.append(pltpu.make_async_copy(notes_ref, dest, sems.at[2 * count]))
        outs[-1].start()
        for copy in outs:
            copy.wait()

    smem = pl.BlockSpec(memory_space=pltpu.SMEM)
    return pl.pallas_call(
        kernel,
        out_shape=jax.ShapeDtypeStruct((peers, held * size + extra, size), tile_data.dtype),
        in_specs=[smem, smem, pl.BlockSpec(memory_space=pltpu.HBM)],
        out_specs=pl.BlockSpec(memory_space=pltpu.HBM),
        scratch_shapes=[
            pltpu.VMEM(tile_data.shape, tile_data.dtype),
            pltpu.VMEM((peers, extra, size), tile_data.dtype),
            pltpu.SMEM((rows * his * los,), jnp.int32),
            pltpu.SemaphoreType.DMA((2 * count + 1,)),
        ],
        compiler_params=params(60 * 2**20),
    )(owner, spot, tile_data)


def each_tile(meta_ref, inbox_ref, tiles_ref, terms_ref, sems, product, add, ready):
    held, size, depth = meta_ref.shape[1], terms_ref.shape[2], tiles_ref.shape[0]
    peers = meta_ref.shape[0]

    def copy(peer):
        at = peer % depth
        rows = pl.ds(0, held * size)
        return pltpu.make_async_copy(inbox_ref.at[peer, rows], tiles_ref.at[at], sems.at[at])

    if sems is not None:
        for peer in range(depth):
            copy(peer).start()
    ready()

    def step(peer, carry):
        if sems is not None:
            copy(peer).wait()
        for slot in range(held):
            spot = jnp.maximum(meta_ref[peer, slot] - 1, 0)
            tile = tiles_ref[peer % depth, slot * size : (slot + 1) * size]
            terms_ref[slot] = product(slot, spot, tile)
        for slot in range(held):
            spot = meta_ref[peer, slot] - 1

            @pl.when(spot >= 0)
            def _():
                add(slot, spot)

        if depth < peers:

            @pl.when(peer + depth < peers)
            def _():
                copy(peer + depth).start()

        return carry

    lax.fori_loop(0, peers, step, 0)


def hbm():
    return pl.BlockSpec(memory_space=pltpu.HBM)


def vmem():
    return pl.BlockSpec(memory_space=pltpu.VMEM)


def smem():
    return pl.BlockSpec(memory_space=pltpu.SMEM)


def join(pieces, me, his):
    part, length = pieces[0].shape

    def kernel(me_ref, *refs):
        for side in range(2):
            rows = pl.ds(pl.multiple_of((me_ref[1] ^ side) * part, part), part)
            for j in range(his):
                refs[-1][j, rows, :] = refs[side * his + j][...]

    return pl.pallas_call(
        kernel,
        out_shape=jax.ShapeDtypeStruct((his, 2 * part, length), pieces[0].dtype),
        in_specs=[smem()] + [vmem()] * len(pieces),
        out_specs=vmem(),
        compiler_params=params(),
    )(me, *pieces)


def row_products(inbox, meta, me, panels, his, los, width):
    peers, size, held = inbox.shape[0], inbox.shape[2], meta.shape[1]
    _, rank, length = panels.shape
    per_chunk = width // size
    keep = peers <= DEPTH

    def kernel(meta_ref, me_ref, inbox_ref, panel_ref, *refs):
        top_ref, bot_ref, tiles_ref, terms_ref, sems = refs
        my_hi, my_lo = me_ref[2], me_ref[3]

        def ready():
            top_ref[...] = jnp.zeros_like(top_ref)
            bot_ref[...] = jnp.zeros_like(bot_ref)

        def product(slot, spot, tile):
            place = pl.ds(pl.multiple_of((spot % CT) * size, size), size)
            panel = panel_ref[slot // CAP ^ my_hi, :, place]
            return lax.dot_general(panel, tile, (((1,), (1,)), ((), ())), preferred_element_type=F32)

        def add(slot, spot):
            trow = spot // CT
            chunk = trow // per_chunk
            lanes = pl.ds(pl.multiple_of((trow % per_chunk) * size, size), size)
            hi, lo = chunk // los ^ my_hi, chunk % los ^ my_lo
            top_ref[lo, hi, :, lanes] += terms_ref[slot, :CUT]
            bot_ref[hi, lo, :, lanes] += terms_ref[slot, CUT:]

        each_tile(meta_ref, inbox_ref, tiles_ref, terms_ref, sems, product, add, ready)

    out_shape = [
        jax.ShapeDtypeStruct((los, his, CUT, width), F32),
        jax.ShapeDtypeStruct((his, los, rank - CUT, width), F32),
    ]
    tiles = (min(peers, DEPTH), held * size, size)
    out_tiles = [jax.ShapeDtypeStruct(tiles, inbox.dtype)] if keep else []
    return pl.pallas_call(
        kernel,
        out_shape=out_shape + out_tiles,
        in_specs=[smem(), smem(), hbm(), vmem()],
        out_specs=[vmem()] * (2 + keep),
        scratch_shapes=([] if keep else [pltpu.VMEM(tiles, inbox.dtype)])
        + [
            pltpu.VMEM((held, rank, size), F32),
            pltpu.SemaphoreType.DMA((tiles[0],)),
        ],
        compiler_params=params(),
    )(meta, me, inbox, panels)


def column_products(inbox, kept, meta, me, pieces, his, los, fars, out_width):
    peers, size, held = inbox.shape[0], inbox.shape[2], meta.shape[1]
    rank, width = pieces[0].shape
    per_chunk, per_out = width // size, out_width // size
    chunks = his * los

    def kernel(meta_ref, me_ref, source_ref, *refs):
        piece_refs, outs = refs[:chunks], refs[chunks : chunks + 4]
        panel_ref, terms_ref, *rest = refs[chunks + 4 :]
        tiles_ref, sems = (source_ref, None) if kept else rest
        my_far, my_core, my_hi, my_lo = (me_ref[i] for i in range(4))

        def ready():
            for out in outs:
                out[...] = jnp.zeros_like(out)
            gram = jnp.zeros((rank, rank), F32)
            for j in range(chunks):
                piece = piece_refs[j][...]
                panel_ref[j] = piece
                gram += lax.dot_general(
                    piece, piece, (((1,), (1,)), ((), ())), preferred_element_type=F32
                )
            shape = (rank, rank)
            diag = lax.broadcasted_iota(jnp.int32, shape, 0) == lax.broadcasted_iota(jnp.int32, shape, 1)
            norms = jnp.sum(jnp.where(diag, gram, 0.0), axis=1, keepdims=True)[CUT:]
            lines = rank * rank // out_width
            for out in (outs[1], outs[3]):
                out[his * fars] = jnp.broadcast_to(norms, out.shape[1:])
                for j in range(rank // lines):
                    out[his * fars + 1, :lines, j * rank : (j + 1) * rank] = gram[j * lines : (j + 1) * lines]

        def product(slot, spot, tile):
            trow = spot // CT
            chunk = trow // per_chunk
            lanes = pl.ds(pl.multiple_of((trow % per_chunk) * size, size), size)
            panel = panel_ref[(chunk // los ^ my_hi) * los + (chunk % los ^ my_lo), :, lanes]
            return lax.dot_general(panel, tile, (((1,), (0,)), ((), ())), preferred_element_type=F32)

        def add(slot, spot):
            tcol = spot % CT
            owner = tcol // per_out
            place = pl.ds(pl.multiple_of((tcol % per_out) * size, size), size)
            far, hi = owner // 2 ^ my_far, slot // CAP ^ my_hi
            for side, (top_ref, bot_ref) in enumerate((outs[:2], outs[2:])):

                @pl.when((owner ^ my_core) % 2 == side)
                def _():
                    top_ref[far, hi, :, place] += terms_ref[slot, :CUT]
                    bot_ref[hi * fars + far, :, place] += terms_ref[slot, CUT:]

        each_tile(meta_ref, source_ref, tiles_ref, terms_ref, sems, product, add, ready)

    tops, bots = (fars, his, CUT, out_width), (his * fars + 2, rank - CUT, out_width)
    out_shape = [tops, bots, tops, bots]
    scratch = [
        pltpu.VMEM((chunks, rank, width), jnp.bfloat16),
        pltpu.VMEM((held, rank, size), F32),
    ]
    if not kept:
        scratch.append(pltpu.VMEM((DEPTH, held * size, size), inbox.dtype))
        scratch.append(pltpu.SemaphoreType.DMA((DEPTH,)))
    return pl.pallas_call(
        kernel,
        out_shape=[jax.ShapeDtypeStruct(shape, F32) for shape in out_shape],
        in_specs=[smem(), smem(), vmem() if kept else hbm()] + [vmem()] * chunks,
        out_specs=[vmem()] * len(out_shape),
        scratch_shapes=scratch,
        compiler_params=params(),
    )(meta, me, *(kept or [inbox]), *pieces)


def assemble(pieces, place, turned):
    count = len(pieces)
    rank, width = pieces[0].shape if turned else pieces[0].shape[::-1]

    def kernel(place_ref, *refs):
        for j in range(count):
            piece = refs[j][...].astype(F32)
            refs[-1][j ^ place_ref[0]] = jnp.transpose(piece) if turned else piece

    return pl.pallas_call(
        kernel,
        out_shape=jax.ShapeDtypeStruct((count, width, rank), F32),
        in_specs=[pl.BlockSpec(memory_space=pltpu.SMEM)]
        + [pl.BlockSpec(memory_space=pltpu.VMEM)] * count,
        out_specs=pl.BlockSpec(memory_space=pltpu.VMEM),
        compiler_params=params(),
    )(place, *pieces).reshape(count * width, rank)


def prepare(factor, gram):
    rank, width = factor.shape

    def kernel(factor_ref, gram_ref, part_ref, mixed_ref, over_ref):
        gram = gram_ref[...]
        shape = (rank, rank)
        diag = lax.broadcasted_iota(jnp.int32, shape, 0) == lax.broadcasted_iota(jnp.int32, shape, 1)
        over = 1.0 / (jnp.sum(jnp.where(diag, gram, 0.0), axis=1, keepdims=True) + RIDGE)
        mixed = gram * over
        mixed_ref[...] = mixed
        over_ref[...] = jnp.broadcast_to(over, shape)
        part_ref[...] = jnp.dot(
            jnp.where(diag, 0.0, mixed), factor_ref[...], precision=HIGH, preferred_element_type=F32
        )

    return pl.pallas_call(
        kernel,
        out_shape=[
            jax.ShapeDtypeStruct((rank, width), F32),
            jax.ShapeDtypeStruct((rank, rank), F32),
            jax.ShapeDtypeStruct((rank, rank), F32),
        ],
        compiler_params=params(),
    )(factor, gram)


def sweep_block(factor, top, bottom, part, mixed, over):
    rank = factor.shape[0]
    product = jnp.concatenate([top, bottom], axis=0)
    over = over[:, :1]
    ahead = []
    for lead in range(0, rank, STEP):
        here = slice(lead, lead + STEP)
        ahead.append(product[here] * over[here] - part[here])
    outs = []
    for b in range(rank // STEP):
        here = slice(b * STEP, (b + 1) * STEP)
        before, block, left = factor[here], mixed[here, here], ahead[b]
        news, moves = [], []
        for k in range(STEP):
            new = jnp.maximum(left[k : k + 1], EPS)
            move = new - before[k : k + 1]
            news.append(new)
            moves.append(move)
            if k + 1 < STEP:
                left = left - block[:, k : k + 1] * move
        outs.append(jnp.concatenate(news, axis=0))
        moved = jnp.concatenate(moves, axis=0)
        for c in range(b + 1, rank // STEP):
            ahead[c] -= jnp.dot(
                mixed[c * STEP : (c + 1) * STEP, here], moved, precision=HIGH, preferred_element_type=F32
            )
    return jnp.concatenate(outs, axis=0)


def sweep(factor, top, bottom, prepared, turned):
    rank, width = factor.shape

    def kernel(*refs):
        new = sweep_block(*(ref[...] for ref in refs[:-1]))
        refs[-1][...] = (jnp.transpose(new) if turned else new).astype(jnp.bfloat16)

    shape = (width, rank) if turned else (rank, width)
    return pl.pallas_call(
        kernel, out_shape=jax.ShapeDtypeStruct(shape, jnp.bfloat16), compiler_params=params()
    )(factor, top, bottom, *prepared)


def swap(x, axis, bit):
    size = lax.axis_size(axis)
    return lax.ppermute(x, axis, [(i, i ^ bit) for i in range(size)])


def bits(axis):
    bit = 1
    while bit < lax.axis_size(axis):
        yield bit
        bit *= 2


def everywhere(x, axes, combine):
    for axis in axes:
        for bit in bits(axis):
            x = combine(x, swap(x, axis, bit))
    return x


def spread(pieces, axis):
    return [
        piece if j == 0 else swap(piece, axis, j)
        for piece in pieces
        for j in range(lax.axis_size(axis))
    ]


def gather(sums, axis, up, down):
    total = sums[0]
    for j in range(1, lax.axis_size(axis)):
        total = total + swap((sums[j] * up).astype(LINK), axis, j).astype(F32) * down
    return total


def bound(squares, terms, size):
    return jnp.sqrt(jnp.maximum(squares, 1e-24)) * (terms * PEAK * size**0.5 / 32768.0)


def scales(gram, terms, size):
    rank = gram.shape[0]
    down = bound(jnp.sum(gram * jnp.eye(rank, dtype=F32), axis=1, keepdims=True), terms, size)
    return [(1.0 / d, d) for d in (down[:CUT], down[CUT:])]


def local(tile_data, owner_ids, tile_spot, w_init, h_init):
    row_axes, col_axes = ("far", "core"), ("hi", "lo")
    fars, cores = lax.axis_size("far"), lax.axis_size("core")
    his, los = lax.axis_size("hi"), lax.axis_size("lo")
    rows, cols = fars * cores, his * los
    slots = rows * cols * CAP
    size, rank = tile_data.shape[1], w_init.shape[1]
    width, length = w_init.shape[0] // cols, h_init.shape[0] // rows
    my_row, my_col = lax.axis_index(row_axes), lax.axis_index(col_axes)
    core = lax.axis_index("core")
    me = jnp.stack([lax.axis_index(a) for a in row_axes + col_axes]).astype(jnp.int32)

    plane = ("far", "core", "lo")
    held = his * CAP
    outbox = pack(owner_ids[:, 0], tile_spot, tile_data, rows, his, los)
    outbox, h_init = lax.optimization_barrier((outbox, h_init))
    inbox = lax.all_to_all(outbox, plane, split_axis=0, concat_axis=0, tiled=True)
    meta = inbox[:, held * size, :held].astype(F32).astype(jnp.int32)

    h_t = h_init.T
    piece = lax.dynamic_slice_in_dim(h_t, core * (rank // 2), rank // 2, 0).astype(jnp.bfloat16)
    pieces = spread([piece], "hi")
    w_t = lax.dynamic_slice_in_dim(w_init, my_col * width, width, 0).T
    own_t = lax.dynamic_slice_in_dim(h_init, my_row * length, length, 0).T
    w_t, own_t, *pieces = lax.optimization_barrier((w_t, own_t, *pieces))
    pieces += [swap(piece, "core", 1) for piece in pieces]

    panels = join(pieces, me, his)
    h_t, panels = lax.optimization_barrier((h_t, panels))
    gram_h = lax.dot_general(h_t, h_t, (((1,), (1,)), ((), ())), precision=HIGH)
    gram_h = everywhere(gram_h, ("hi",), jnp.add)
    gram_h, meta = lax.optimization_barrier((gram_h, meta))
    gram_h = everywhere(gram_h, ("lo",), jnp.add)
    prepared = prepare(w_t, gram_h)
    parts = row_products(inbox, meta, me, panels, his, los, width)
    parts, kept = parts[:2], parts[2:]
    high, low = scales(gram_h, slots * cols, size)
    top = gather(gather(parts[0], "lo", *high), "hi", *high)
    bottom = gather(gather(parts[1], "hi", *low), "lo", *low)
    w_low = sweep(w_t, top, bottom, prepared, False)
    pieces = spread(spread([w_low], "hi"), "lo")

    parts = column_products(inbox, kept, meta, me, pieces, his, los, fars, length)

    bottom = parts[1] + swap(parts[3], "core", 1)
    bottom, away = lax.optimization_barrier((bottom, parts[2]))
    top = parts[0] + swap(away, "core", 1)
    lines = rank * rank // length
    gram_w = bottom[-1, :lines].reshape(lines, length // rank, rank)
    gram_w = gram_w.transpose(1, 0, 2).reshape(rank, rank)
    down = bound(bottom[-2], slots * 2, size)
    bottom = bottom[:-2].reshape(his, fars, *bottom.shape[1:])
    sends = [(bottom[j] * (1.0 / down)).astype(LINK) for j in range(1, his)]
    *sends, gram_w = lax.optimization_barrier((*sends, gram_w))
    gram_w = everywhere(gram_w, ("far",), jnp.add)
    prepared = prepare(own_t, gram_w)
    high, low = scales(gram_w, slots * rows * his, size)
    bottom = bottom[0]
    for j, send in enumerate(sends, 1):
        bottom = bottom + swap(send, "hi", j).astype(F32) * down
    bottom = gather(bottom, "far", *low)
    top = gather(gather(top, "far", *high), "hi", *high)
    h_low = sweep(own_t, top, bottom, prepared, True)
    h_low, *pieces = lax.optimization_barrier((h_low, *pieces))
    w_new = assemble(pieces, my_col[None].astype(jnp.int32), True)
    pieces = spread([h_low], "far")
    pieces[0], w_new = lax.optimization_barrier((pieces[0], w_new))
    h_new = assemble(spread(pieces, "core"), my_row[None].astype(jnp.int32), False)
    return w_new, h_new


def solution(mesh):
    rows, cols = mesh.shape["row"], mesh.shape["col"]
    his = 4 if cols % 4 == 0 else 1
    shape = (rows // 2, 2, his, cols // his)
    fine = Mesh(mesh.devices.reshape(shape), ("far", "core", "hi", "lo"))
    row, col = ("far", "core"), ("hi", "lo")
    in_specs = (P(row + col, None, None), P(row + col, None), P(row + col), P(row, None), P(col, None))
    out_specs = (P(row, None), P(col, None))
    return jax.shard_map(local, mesh=fine, in_specs=in_specs, out_specs=out_specs, check_vma=False)
```

```python
import jax
import jax.numpy as jnp
from jax import lax
from jax.experimental import pallas as pl
from jax.experimental.pallas import tpu as pltpu
from jax.sharding import Mesh
from jax.sharding import PartitionSpec as P

CT = 16
CAP = 2
EPS = 1e-06
RIDGE = 1.0
HIGH = lax.Precision.HIGHEST
F32 = jnp.float32
LINK = jnp.float16
STEP = 32
DEPTH = 8
BATCH = 2
PEAK = 256.0
CUT = 80
VMEM_LIMIT = 24 * 2**20


def params(limit=VMEM_LIMIT):
    return pltpu.CompilerParams(vmem_limit_bytes=limit)


def pack(owner, spot, tile_data, rows, his, los):
    count, size = tile_data.shape[0], tile_data.shape[1]
    peers, held, extra = rows * los, his * CAP, 16

    def kernel(owner_ref, spot_ref, tiles_ref, out_ref, held_ref, notes_ref, seen_ref, sems):
        ins = [
            pltpu.make_async_copy(tiles_ref.at[s], held_ref.at[s], sems.at[s]) for s in range(count)
        ]
        for copy in ins:
            copy.start()

        def clear(i, carry):
            seen_ref[i] = 0
            return carry

        lax.fori_loop(0, rows * his * los, clear, 0)
        shape = (peers, size)
        peer_of = lax.broadcasted_iota(jnp.int32, shape, 0)
        slot_of = lax.broadcasted_iota(jnp.int32, shape, 1)
        notes = jnp.zeros(shape, F32)
        outs = []
        for s in range(count):
            one = owner_ref[s]
            row, col = one // (his * los), one % (his * los)
            peer, slot = row * los + col % los, col // los * CAP + seen_ref[one]
            seen_ref[one] += 1
            notes = jnp.where((peer_of == peer) & (slot_of == slot), (spot_ref[s] + 1).astype(F32), notes)
            dest = out_ref.at[peer, pl.ds(pl.multiple_of(slot * size, size), size)]
            ins[s].wait()
            outs.append(pltpu.make_async_copy(held_ref.at[s], dest, sems.at[count + s]))
            outs[-1].start()
        for peer in range(peers):
            line = jnp.broadcast_to(notes[peer : peer + 1], (extra, size))
            notes_ref[peer] = line.astype(notes_ref.dtype)
        dest = out_ref.at[:, pl.ds(held * size, extra)]
        outs.append(pltpu.make_async_copy(notes_ref, dest, sems.at[2 * count]))
        outs[-1].start()
        for copy in outs:
            copy.wait()

    smem = pl.BlockSpec(memory_space=pltpu.SMEM)
    return pl.pallas_call(
        kernel,
        out_shape=jax.ShapeDtypeStruct((peers, held * size + extra, size), tile_data.dtype),
        in_specs=[smem, smem, pl.BlockSpec(memory_space=pltpu.HBM)],
        out_specs=pl.BlockSpec(memory_space=pltpu.HBM),
        scratch_shapes=[
            pltpu.VMEM(tile_data.shape, tile_data.dtype),
            pltpu.VMEM((peers, extra, size), tile_data.dtype),
            pltpu.SMEM((rows * his * los,), jnp.int32),
            pltpu.SemaphoreType.DMA((2 * count + 1,)),
        ],
        compiler_params=params(60 * 2**20),
    )(owner, spot, tile_data)


def each_tile(meta_ref, inbox_ref, tiles_ref, terms_ref, sems, product, add, ready):
    held, size, depth = meta_ref.shape[1], terms_ref.shape[2], tiles_ref.shape[0]
    peers = meta_ref.shape[0]

    def copy(peer):
        at = peer % depth
        rows = pl.ds(0, held * size)
        return pltpu.make_async_copy(inbox_ref.at[peer, rows], tiles_ref.at[at], sems.at[at])

    if sems is not None:
        for peer in range(depth):
            copy(peer).start()
    ready()

    def step(turn, carry):
        first = turn * BATCH
        if sems is not None:
            for b in range(BATCH):
                copy(first + b).wait()
        for b in range(BATCH):
            for slot in range(held):
                spot = jnp.maximum(meta_ref[first + b, slot] - 1, 0)
                tile = tiles_ref[(first + b) % depth, slot * size : (slot + 1) * size]
                terms_ref[b * held + slot] = product(slot, spot, tile)
        for b in range(BATCH):
            for slot in range(held):
                spot = meta_ref[first + b, slot] - 1

                @pl.when(spot >= 0)
                def _():
                    add(slot, spot, b * held + slot)

        if depth < peers:
            for b in range(BATCH):

                @pl.when(first + b + depth < peers)
                def _():
                    copy(first + b + depth).start()

        return carry

    lax.fori_loop(0, peers // BATCH, step, 0)


def hbm():
    return pl.BlockSpec(memory_space=pltpu.HBM)


def vmem():
    return pl.BlockSpec(memory_space=pltpu.VMEM)


def smem():
    return pl.BlockSpec(memory_space=pltpu.SMEM)


def join(pieces, me, his):
    part, length = pieces[0].shape

    def kernel(me_ref, *refs):
        for side in range(2):
            rows = pl.ds(pl.multiple_of((me_ref[1] ^ side) * part, part), part)
            for j in range(his):
                refs[-1][j, rows, :] = refs[side * his + j][...]

    return pl.pallas_call(
        kernel,
        out_shape=jax.ShapeDtypeStruct((his, 2 * part, length), pieces[0].dtype),
        in_specs=[smem()] + [vmem()] * len(pieces),
        out_specs=vmem(),
        compiler_params=params(),
    )(me, *pieces)


def row_products(inbox, meta, me, panels, his, los, width):
    peers, size, held = inbox.shape[0], inbox.shape[2], meta.shape[1]
    _, rank, length = panels.shape
    per_chunk = width // size
    keep = peers <= DEPTH

    def kernel(meta_ref, me_ref, inbox_ref, panel_ref, *refs):
        top_ref, bot_ref, tiles_ref, terms_ref, sems = refs
        my_hi, my_lo = me_ref[2], me_ref[3]

        def ready():
            top_ref[...] = jnp.zeros_like(top_ref)
            bot_ref[...] = jnp.zeros_like(bot_ref)

        def product(slot, spot, tile):
            place = pl.ds(pl.multiple_of((spot % CT) * size, size), size)
            panel = panel_ref[slot // CAP ^ my_hi, :, place]
            return lax.dot_general(panel, tile, (((1,), (1,)), ((), ())), preferred_element_type=F32)

        def add(slot, spot, at):
            trow = spot // CT
            chunk = trow // per_chunk
            lanes = pl.ds(pl.multiple_of((trow % per_chunk) * size, size), size)
            hi, lo = chunk // los ^ my_hi, chunk % los ^ my_lo
            top_ref[lo, hi, :, lanes] += terms_ref[at, :CUT]
            bot_ref[hi, lo, :, lanes] += terms_ref[at, CUT:]

        each_tile(meta_ref, inbox_ref, tiles_ref, terms_ref, sems, product, add, ready)

    out_shape = [
        jax.ShapeDtypeStruct((los, his, CUT, width), F32),
        jax.ShapeDtypeStruct((his, los, rank - CUT, width), F32),
    ]
    tiles = (min(peers, DEPTH), held * size, size)
    out_tiles = [jax.ShapeDtypeStruct(tiles, inbox.dtype)] if keep else []
    return pl.pallas_call(
        kernel,
        out_shape=out_shape + out_tiles,
        in_specs=[smem(), smem(), hbm(), vmem()],
        out_specs=[vmem()] * (2 + keep),
        scratch_shapes=([] if keep else [pltpu.VMEM(tiles, inbox.dtype)])
        + [
            pltpu.VMEM((BATCH * held, rank, size), F32),
            pltpu.SemaphoreType.DMA((tiles[0],)),
        ],
        compiler_params=params(),
    )(meta, me, inbox, panels)


def column_products(inbox, kept, meta, me, pieces, his, los, fars, out_width):
    peers, size, held = inbox.shape[0], inbox.shape[2], meta.shape[1]
    rank, width = pieces[0].shape
    per_chunk, per_out = width // size, out_width // size
    chunks = his * los

    def kernel(meta_ref, me_ref, source_ref, *refs):
        piece_refs, outs = refs[:chunks], refs[chunks : chunks + 4]
        panel_ref, terms_ref, *rest = refs[chunks + 4 :]
        tiles_ref, sems = (source_ref, None) if kept else rest
        my_far, my_core, my_hi, my_lo = (me_ref[i] for i in range(4))

        def ready():
            for out in outs:
                out[...] = jnp.zeros_like(out)
            gram = jnp.zeros((rank, rank), F32)
            for j in range(chunks):
                piece = piece_refs[j][...]
                panel_ref[j] = piece
                gram += lax.dot_general(
                    piece, piece, (((1,), (1,)), ((), ())), preferred_element_type=F32
                )
            shape = (rank, rank)
            diag = lax.broadcasted_iota(jnp.int32, shape, 0) == lax.broadcasted_iota(jnp.int32, shape, 1)
            norms = jnp.sum(jnp.where(diag, gram, 0.0), axis=1, keepdims=True)[CUT:]
            lines = rank * rank // out_width
            for out in (outs[1], outs[3]):
                out[his * fars] = jnp.broadcast_to(norms, out.shape[1:])
                for j in range(rank // lines):
                    out[his * fars + 1, :lines, j * rank : (j + 1) * rank] = gram[j * lines : (j + 1) * lines]

        def product(slot, spot, tile):
            trow = spot // CT
            chunk = trow // per_chunk
            lanes = pl.ds(pl.multiple_of((trow % per_chunk) * size, size), size)
            panel = panel_ref[(chunk // los ^ my_hi) * los + (chunk % los ^ my_lo), :, lanes]
            return lax.dot_general(panel, tile, (((1,), (0,)), ((), ())), preferred_element_type=F32)

        def add(slot, spot, at):
            tcol = spot % CT
            owner = tcol // per_out
            place = pl.ds(pl.multiple_of((tcol % per_out) * size, size), size)
            far, hi = owner // 2 ^ my_far, slot // CAP ^ my_hi
            for side, (top_ref, bot_ref) in enumerate((outs[:2], outs[2:])):

                @pl.when((owner ^ my_core) % 2 == side)
                def _():
                    top_ref[far, hi, :, place] += terms_ref[at, :CUT]
                    bot_ref[hi * fars + far, :, place] += terms_ref[at, CUT:]

        each_tile(meta_ref, source_ref, tiles_ref, terms_ref, sems, product, add, ready)

    tops, bots = (fars, his, CUT, out_width), (his * fars + 2, rank - CUT, out_width)
    out_shape = [tops, bots, tops, bots]
    scratch = [
        pltpu.VMEM((chunks, rank, width), jnp.bfloat16),
        pltpu.VMEM((BATCH * held, rank, size), F32),
    ]
    if not kept:
        scratch.append(pltpu.VMEM((DEPTH, held * size, size), inbox.dtype))
        scratch.append(pltpu.SemaphoreType.DMA((DEPTH,)))
    return pl.pallas_call(
        kernel,
        out_shape=[jax.ShapeDtypeStruct(shape, F32) for shape in out_shape],
        in_specs=[smem(), smem(), vmem() if kept else hbm()] + [vmem()] * chunks,
        out_specs=[vmem()] * len(out_shape),
        scratch_shapes=scratch,
        compiler_params=params(),
    )(meta, me, *(kept or [inbox]), *pieces)


def assemble(pieces, place, turned):
    count = len(pieces)
    rank, width = pieces[0].shape if turned else pieces[0].shape[::-1]

    def kernel(place_ref, *refs):
        for j in range(count):
            piece = refs[j][...].astype(F32)
            refs[-1][j ^ place_ref[0]] = jnp.transpose(piece) if turned else piece

    return pl.pallas_call(
        kernel,
        out_shape=jax.ShapeDtypeStruct((count, width, rank), F32),
        in_specs=[pl.BlockSpec(memory_space=pltpu.SMEM)]
        + [pl.BlockSpec(memory_space=pltpu.VMEM)] * count,
        out_specs=pl.BlockSpec(memory_space=pltpu.VMEM),
        compiler_params=params(),
    )(place, *pieces).reshape(count * width, rank)


def prepare(factor, gram):
    rank, width = factor.shape

    def kernel(factor_ref, gram_ref, part_ref, mixed_ref, over_ref):
        gram = gram_ref[...]
        shape = (rank, rank)
        diag = lax.broadcasted_iota(jnp.int32, shape, 0) == lax.broadcasted_iota(jnp.int32, shape, 1)
        over = 1.0 / (jnp.sum(jnp.where(diag, gram, 0.0), axis=1, keepdims=True) + RIDGE)
        mixed = gram * over
        mixed_ref[...] = mixed
        over_ref[...] = jnp.broadcast_to(over, shape)
        part_ref[...] = jnp.dot(
            jnp.where(diag, 0.0, mixed), factor_ref[...], precision=HIGH, preferred_element_type=F32
        )

    return pl.pallas_call(
        kernel,
        out_shape=[
            jax.ShapeDtypeStruct((rank, width), F32),
            jax.ShapeDtypeStruct((rank, rank), F32),
            jax.ShapeDtypeStruct((rank, rank), F32),
        ],
        compiler_params=params(),
    )(factor, gram)


def sweep_block(factor, top, bottom, part, mixed, over):
    rank = factor.shape[0]
    product = jnp.concatenate([top, bottom], axis=0)
    over = over[:, :1]
    ahead = []
    for lead in range(0, rank, STEP):
        here = slice(lead, lead + STEP)
        ahead.append(product[here] * over[here] - part[here])
    outs = []
    for b in range(rank // STEP):
        here = slice(b * STEP, (b + 1) * STEP)
        before, block, left = factor[here], mixed[here, here], ahead[b]
        news, moves = [], []
        for k in range(STEP):
            new = jnp.maximum(left[k : k + 1], EPS)
            move = new - before[k : k + 1]
            news.append(new)
            moves.append(move)
            if k + 1 < STEP:
                left = left - block[:, k : k + 1] * move
        outs.append(jnp.concatenate(news, axis=0))
        moved = jnp.concatenate(moves, axis=0)
        for c in range(b + 1, rank // STEP):
            ahead[c] -= jnp.dot(
                mixed[c * STEP : (c + 1) * STEP, here], moved, precision=HIGH, preferred_element_type=F32
            )
    return jnp.concatenate(outs, axis=0)


def sweep(factor, top, bottom, prepared, turned):
    rank, width = factor.shape

    def kernel(*refs):
        new = sweep_block(*(ref[...] for ref in refs[:-1]))
        refs[-1][...] = (jnp.transpose(new) if turned else new).astype(jnp.bfloat16)

    shape = (width, rank) if turned else (rank, width)
    return pl.pallas_call(
        kernel, out_shape=jax.ShapeDtypeStruct(shape, jnp.bfloat16), compiler_params=params()
    )(factor, top, bottom, *prepared)


def swap(x, axis, bit):
    size = lax.axis_size(axis)
    return lax.ppermute(x, axis, [(i, i ^ bit) for i in range(size)])


def bits(axis):
    bit = 1
    while bit < lax.axis_size(axis):
        yield bit
        bit *= 2


def everywhere(x, axes, combine):
    for axis in axes:
        for bit in bits(axis):
            x = combine(x, swap(x, axis, bit))
    return x


def spread(pieces, axis):
    return [
        piece if j == 0 else swap(piece, axis, j)
        for piece in pieces
        for j in range(lax.axis_size(axis))
    ]


def gather(sums, axis, up, down):
    total = sums[0]
    for j in range(1, lax.axis_size(axis)):
        total = total + swap((sums[j] * up).astype(LINK), axis, j).astype(F32) * down
    return total


def bound(squares, terms, size):
    return jnp.sqrt(jnp.maximum(squares, 1e-24)) * (terms * PEAK * size**0.5 / 32768.0)


def scales(gram, terms, size):
    rank = gram.shape[0]
    down = bound(jnp.sum(gram * jnp.eye(rank, dtype=F32), axis=1, keepdims=True), terms, size)
    return [(1.0 / d, d) for d in (down[:CUT], down[CUT:])]


def local(tile_data, owner_ids, tile_spot, w_init, h_init):
    row_axes, col_axes = ("far", "core"), ("hi", "lo")
    fars, cores = lax.axis_size("far"), lax.axis_size("core")
    his, los = lax.axis_size("hi"), lax.axis_size("lo")
    rows, cols = fars * cores, his * los
    slots = rows * cols * CAP
    size, rank = tile_data.shape[1], w_init.shape[1]
    width, length = w_init.shape[0] // cols, h_init.shape[0] // rows
    my_row, my_col = lax.axis_index(row_axes), lax.axis_index(col_axes)
    core = lax.axis_index("core")
    me = jnp.stack([lax.axis_index(a) for a in row_axes + col_axes]).astype(jnp.int32)

    plane = ("far", "core", "lo")
    held = his * CAP
    outbox = pack(owner_ids[:, 0], tile_spot, tile_data, rows, his, los)
    outbox, h_init = lax.optimization_barrier((outbox, h_init))
    inbox = lax.all_to_all(outbox, plane, split_axis=0, concat_axis=0, tiled=True)
    meta = inbox[:, held * size, :held].astype(F32).astype(jnp.int32)

    h_t = h_init.T
    piece = lax.dynamic_slice_in_dim(h_t, core * (rank // 2), rank // 2, 0).astype(jnp.bfloat16)
    pieces = spread([piece], "hi")
    w_t = lax.dynamic_slice_in_dim(w_init, my_col * width, width, 0).T
    own_t = lax.dynamic_slice_in_dim(h_init, my_row * length, length, 0).T
    w_t, own_t, *pieces = lax.optimization_barrier((w_t, own_t, *pieces))
    pieces += [swap(piece, "core", 1) for piece in pieces]

    panels = join(pieces, me, his)
    h_t, panels = lax.optimization_barrier((h_t, panels))
    gram_h = lax.dot_general(h_t, h_t, (((1,), (1,)), ((), ())), precision=HIGH)
    gram_h = everywhere(gram_h, ("hi",), jnp.add)
    gram_h, meta = lax.optimization_barrier((gram_h, meta))
    gram_h = everywhere(gram_h, ("lo",), jnp.add)
    prepared = prepare(w_t, gram_h)
    parts = row_products(inbox, meta, me, panels, his, los, width)
    parts, kept = parts[:2], parts[2:]
    high, low = scales(gram_h, slots * cols, size)
    top = gather(gather(parts[0], "lo", *high), "hi", *high)
    bottom = gather(gather(parts[1], "hi", *low), "lo", *low)
    w_low = sweep(w_t, top, bottom, prepared, False)
    pieces = spread(spread([w_low], "hi"), "lo")

    parts = column_products(inbox, kept, meta, me, pieces, his, los, fars, length)

    bottom = parts[1] + swap(parts[3], "core", 1)
    bottom, away = lax.optimization_barrier((bottom, parts[2]))
    top = parts[0] + swap(away, "core", 1)
    lines = rank * rank // length
    gram_w = bottom[-1, :lines].reshape(lines, length // rank, rank)
    gram_w = gram_w.transpose(1, 0, 2).reshape(rank, rank)
    down = bound(bottom[-2], slots * 2, size)
    bottom = bottom[:-2].reshape(his, fars, *bottom.shape[1:])
    sends = [(bottom[j] * (1.0 / down)).astype(LINK) for j in range(1, his)]
    *sends, gram_w = lax.optimization_barrier((*sends, gram_w))
    gram_w = everywhere(gram_w, ("far",), jnp.add)
    prepared = prepare(own_t, gram_w)
    high, low = scales(gram_w, slots * rows * his, size)
    bottom = bottom[0]
    for j, send in enumerate(sends, 1):
        bottom = bottom + swap(send, "hi", j).astype(F32) * down
    bottom = gather(bottom, "far", *low)
    top = gather(gather(top, "far", *high), "hi", *high)
    h_low = sweep(own_t, top, bottom, prepared, True)
    h_low, *pieces = lax.optimization_barrier((h_low, *pieces))
    w_new = assemble(pieces, my_col[None].astype(jnp.int32), True)
    pieces = spread([h_low], "far")
    pieces[0], w_new = lax.optimization_barrier((pieces[0], w_new))
    h_new = assemble(spread(pieces, "core"), my_row[None].astype(jnp.int32), False)
    return w_new, h_new


def solution(mesh):
    rows, cols = mesh.shape["row"], mesh.shape["col"]
    his = 4 if cols % 4 == 0 else 1
    shape = (rows // 2, 2, his, cols // his)
    fine = Mesh(mesh.devices.reshape(shape), ("far", "core", "hi", "lo"))
    row, col = ("far", "core"), ("hi", "lo")
    in_specs = (P(row + col, None, None), P(row + col, None), P(row + col), P(row, None), P(col, None))
    out_specs = (P(row, None), P(col, None))
    return jax.shard_map(local, mesh=fine, in_specs=in_specs, out_specs=out_specs, check_vma=False)
```
